512 devices in a mesh: lat: 32 (over x, z_hi, core), lon: 16 (over z_lo, y).
Axes of the slice: x: 4, y: 4, z: 16 (z_hi: 4, z_lo: 4; z = z_hi * 4 + z_lo), core: 2. Of those that a mesh axis runs over, the one named last changes fastest.
Arguments:
- cotangent: bfloat16 [3, 50, 1536, 4096], P(None, None, 'lat', 'lon'), may hold values from -6 to 6
- wave_order: int32 [512], replicated, may hold values from 0 to 511, each once
- band_diagonal: bfloat16 [512, 24, 4096], P(('lat', 'lon')), may hold values from -0.4375 to 0.4375
- band_lower: bfloat16 [512, 23, 4096], P(('lat', 'lon')), may hold values from -0.4375 to 0.4375
- vertical_matrix: bfloat16 [3, 50, 50], replicated, may hold values from -0.875 to 0.875
Outputs:
- adjoint_spectra: bfloat16 [512, 2, 3, 50, 1536], P(('lat', 'lon'))
The draws below stay inside these ranges and needn't reach their ends.
Inputs may be any that keep to these rules, and one draw needn't show every extreme that they name: `wave_order`: each wavenumber 0 to 511 stands at exactly one slot.
All inputs are finite; a program needn't handle non-finite values.
Results may differ from the reference program's by a relative error of at most 0.0077.
Values may be sent and summed in bfloat16 or wider, within the bound.
A program may use at most 128 MiB of HBM per device.

```python
import math
import jax
import jax.numpy as jnp
from jax import lax

F = 3
LEV = 50
NLON = 4096
NLAT = 1536
BLK = 64
M = 512
KB = 24


def shard_levels(rng, extent, cuts, low, high):
    loudness = 1.0
    for axis_at, parts in cuts:
        draws = jax.random.uniform(jax.random.fold_in(jax.random.fold_in(rng, 6), axis_at), (parts,), jnp.float32, low / len(cuts), high / len(cuts))
        loudness = loudness * jnp.repeat(jnp.exp(draws), extent[axis_at] // parts).reshape((-1,) + (1,) * (len(extent) - 1 - axis_at))
    return loudness


def gaussian(stream_key, extent, deviation, limit, cuts=(), kind=jnp.bfloat16):
    values = jax.random.normal(stream_key, extent, jnp.float32) * deviation
    if len(cuts) > 0:
        values = shard_levels(stream_key, extent, cuts, -0.22, 0.18) * values
    return jnp.clip(values, min=-limit, max=limit).astype(kind)


def setup_inputs(seed: int = 0) -> dict:
    key_list = jax.random.split(jax.random.key(seed), 6)
    return {
        "cotangent": gaussian(key_list[0], (F, LEV, NLAT, NLON), 1.0, 6.0, ((2, 32), (3, 16))),
        "wave_order": jax.random.permutation(key_list[1], M).astype(jnp.int32),
        "band_diagonal": gaussian(key_list[2], (M, KB, BLK * BLK), (3 * BLK) ** -0.5, 0.4375, ((0, 512),)),
        "band_lower": gaussian(key_list[3], (M, KB - 1, BLK * BLK), (3 * BLK) ** -0.5, 0.4375, ((0, 512),)),
        "vertical_matrix": gaussian(key_list[4], (F, LEV, LEV), LEV ** -0.5, 0.875),
    }


def zonal_table(wave_list, grid_lon):
    longitudes = jnp.arange(grid_lon, dtype=jnp.int32)
    phases = longitudes[:, None] * wave_list[None, :].astype(jnp.int32) % grid_lon
    angles = 2.0 * math.pi / grid_lon * phases.astype(jnp.float32)
    table = jnp.stack([jnp.cos(angles), jnp.sin(angles)], axis=-1) * math.sqrt(2.0 / grid_lon)
    return table.reshape(grid_lon, 2 * wave_list.shape[0]).astype(jnp.bfloat16)

def meridional_table(latitudes, grid_lat):
    modes = jnp.arange(grid_lat, dtype=jnp.int32)
    phases = modes[None, :] * (2 * latitudes[:, None].astype(jnp.int32) + 1) % (4 * grid_lat)
    angles = math.pi / (2 * grid_lat) * phases.astype(jnp.float32)
    return (jnp.cos(angles) * math.sqrt(2.0 / grid_lat)).astype(jnp.bfloat16)

def band_apply(blocks, diagonal_blocks, lower_blocks):
    result = jnp.einsum('bij,crbj->crbi', diagonal_blocks, blocks)
    below = jnp.einsum('bij,crbj->crbi', lower_blocks, blocks[:, :, :-1])
    above = jnp.einsum('bji,crbj->crbi', lower_blocks, blocks[:, :, 1:])
    below = jnp.pad(below, ((0, 0), (0, 0), (1, 0), (0, 0)))
    above = jnp.pad(above, ((0, 0), (0, 0), (0, 1), (0, 0)))
    return result + below + above

def reference(cotangent, wave_order, band_diagonal, band_lower, vertical_matrix):
    rows = cotangent.reshape(F * LEV, NLAT, NLON)
    zonal_basis = zonal_table(wave_order, NLON)
    meridional_basis = meridional_table(jnp.arange(NLAT, dtype=jnp.int32), NLAT)

    def transform(grid):
        coeffs = jnp.dot(grid, zonal_basis, preferred_element_type=jnp.float32).astype(jnp.bfloat16)
        return jnp.dot(meridional_basis.T, coeffs, preferred_element_type=jnp.float32).astype(jnp.bfloat16)
    spectra = lax.map(transform, rows)
    spectra = spectra.reshape(F * LEV, NLAT, M, 2).transpose(2, 3, 0, 1)

    def finish(items):
        local, diagonal_flat, lower_flat = items
        diagonal_blocks = diagonal_flat.reshape(KB, BLK, BLK).astype(jnp.float32)
        lower_blocks = lower_flat.reshape(KB - 1, BLK, BLK).astype(jnp.float32)
        blocks = local.astype(jnp.float32).reshape(2, F * LEV, NLAT // BLK, BLK)
        banded = band_apply(blocks, diagonal_blocks, lower_blocks)
        banded = banded.astype(jnp.bfloat16)
        layered = banded.reshape(2, F, LEV, NLAT).astype(jnp.float32)
        mixed = jnp.einsum('flm,cflk->cfmk', vertical_matrix.astype(jnp.float32), layered)
        return mixed.astype(jnp.bfloat16)
    return lax.map(finish, (spectra, band_diagonal, band_lower))
```

```python
import functools
import math

import jax
import jax.numpy as jnp
from jax import lax
from jax.experimental import pallas as pl
from jax.experimental.pallas import tpu as pltpu
from jax.sharding import PartitionSpec as P

BLK = 64
MESH = pl.DeviceIdType.MESH

X, ZHI, CORE, ZLO, Y = 4, 4, 2, 4, 4
PLANE = X * CORE * Y
SIDES, DESTS = 2, 8
GROUP_STEP = ((3, 3, 3, 3, 2, 2, 0, 0), (1, 1, 1, 1, 2, 2, 0, 0))
GROUP_PLACE = ((0, 1, 2, 3, 2, 3, 0, 1), (0, 1, 2, 3, 0, 1, 2, 3))
ROWS = 2
AHEAD = 4


def place():
    lat, lon = lax.axis_index("lat"), lax.axis_index("lon")
    return lat // (ZHI * CORE), lat // CORE % ZHI, lat % CORE, lon // Y, lon % Y


def device(x, hi, core, lo, y):
    return ((x * ZHI + hi) * CORE + core, lo * Y + y)


def zonal_kernel(
    rows, share, steps,
    grid_ref, u_ref, v_ref, cos_ref, sin_ref, out_ref,
    grid, basis, right_in, left_in, right_out, left_out, packed, total,
    grid_sem, grid_send, right_send, right_recv, left_send, left_recv,
    pack_send, out_sem,
):
    x, hi, core, lo, y = place()
    lat_local, lon_local = grid_ref.shape[1:]
    half = basis.shape[1] // 2
    width = half // DESTS

    barrier = pltpu.get_barrier_semaphore()
    for step in range(1, Y):
        pl.semaphore_signal(
            barrier, inc=1, device_id=device(x, hi, core, lo, (y + step) % Y), device_id_type=MESH
        )
    for step in range(1, ZHI * ZLO):
        z = (hi * ZLO + lo + step) % (ZHI * ZLO)
        pl.semaphore_signal(
            barrier, inc=1, device_id=device(x, z // ZLO, core, z % ZLO, y), device_id_type=MESH
        )
    pl.semaphore_wait(barrier, Y - 1 + ZHI * ZLO - 1)

    def first_row(owner):
        return jnp.minimum(owner * share, rows - share)

    def grid_copies(step):
        columns = pl.ds(pl.multiple_of(y * lon_local, lon_local), lon_local)
        target = grid.at[pl.ds(step * ROWS, ROWS), :, columns]
        for offset in range(1, Y):
            owner = (y + offset) % Y
            pltpu.make_async_remote_copy(
                src_ref=grid_ref.at[pl.ds(first_row(owner) + step * ROWS, ROWS)],
                dst_ref=target,
                send_sem=grid_send,
                recv_sem=grid_sem.at[step],
                device_id=device(x, hi, core, lo, owner),
                device_id_type=MESH,
            ).start()
        pltpu.make_async_copy(
            grid_ref.at[pl.ds(first_row(y) + step * ROWS, ROWS)], target, grid_sem.at[step]
        ).start()

    for step in range(AHEAD):
        grid_copies(step)

    coarse, fine = u_ref.shape[0], cos_ref.shape[0]

    def fill(a, carry):
        piece = u_ref[pl.ds(a, 1), :] * cos_ref[...] + v_ref[pl.ds(a, 1), :] * sin_ref[...]
        basis[pl.ds(pl.multiple_of(a * fine, fine), fine), :] = piece.astype(basis.dtype)
        return carry

    lax.fori_loop(0, coarse, fill, 0)

    def product(step, side):
        left = grid[pl.ds(step * ROWS, ROWS)].reshape(ROWS * lat_local, grid.shape[2])
        return jnp.dot(
            left, basis[:, side * half : (side + 1) * half], preferred_element_type=jnp.float32
        )

    def hand_out(step, side):
        for pair in range(DESTS // 2):
            lanes = slice(pair * 2 * width, (pair + 1) * 2 * width)
            top, low = total[:lat_local, lanes], total[lat_local:, lanes]
            for odd in range(2):
                part = slice(odd * width, (odd + 1) * width)
                packed[step, pair * 2 + odd] = jnp.concatenate(
                    [top[:, part], low[:, part]], axis=1
                ).astype(packed.dtype)
        own_lo = ZLO - 1 if side else 0
        for dest in range(DESTS):
            to_hi = (hi + GROUP_STEP[side][dest]) % ZHI
            to_lo = GROUP_PLACE[side][dest]
            if GROUP_STEP[side][dest] == 0 and to_lo == own_lo:
                pltpu.make_async_copy(packed.at[step, dest], out_ref.at[step, hi], out_sem).start()
            else:
                pltpu.make_async_remote_copy(
                    src_ref=packed.at[step, dest],
                    dst_ref=out_ref.at[step, hi],
                    send_sem=pack_send,
                    recv_sem=out_sem,
                    device_id=device(x, to_hi, core, to_lo, y),
                    device_id_type=MESH,
                ).start()

    def chain(step, side):
        arrived, leaving = (right_in, right_out) if side else (left_in, left_out)
        send_sem, recv_sem = (right_send, right_recv) if side else (left_send, left_recv)
        first, last = (0, ZLO - 1) if side else (ZLO - 1, 0)
        total[...] = product(step, side)

        @pl.when(lo != first)
        def _():
            pltpu.make_async_copy(arrived.at[step], arrived.at[step], recv_sem.at[step]).wait()
            total[...] += arrived[step].astype(jnp.float32)

        @pl.when(lo != last)
        def _():
            leaving[step] = total[...].astype(leaving.dtype)
            pltpu.make_async_remote_copy(
                src_ref=leaving.at[step],
                dst_ref=arrived.at[step],
                send_sem=send_sem,
                recv_sem=recv_sem.at[step],
                device_id=device(x, hi, core, lo + (1 if side else -1), y),
                device_id_type=MESH,
            ).start()

        @pl.when(lo == last)
        def _():
            hand_out(step, side)

    def one(step, carry):
        @pl.when(step + AHEAD < steps)
        def _():
            grid_copies(step + AHEAD)

        first = step - jnp.minimum(lo, ZLO - 1 - lo)

        @pl.when((first >= 0) & (first < steps))
        def _():
            block = grid.at[pl.ds(first * ROWS, ROWS)]
            pltpu.make_async_copy(block, block, grid_sem.at[first]).wait()

        for side in range(SIDES):
            at = step - (lo if side else ZLO - 1 - lo)

            @pl.when((at >= 0) & (at < steps))
            def _():
                chain(at, side)

        return carry

    lax.fori_loop(0, steps + ZLO - 1, one, 0)

    sent = grid_ref.at[pl.ds(0, (Y - 1) * share)]
    pltpu.make_async_copy(sent, sent, grid_send).wait()

    @pl.when(lo != ZLO - 1)
    def _():
        pltpu.make_async_copy(right_out, right_out, right_send).wait()

    @pl.when(lo != 0)
    def _():
        pltpu.make_async_copy(left_out, left_out, left_send).wait()

    @pl.when((lo == 0) | (lo == ZLO - 1))
    def _():
        sent = packed.at[:, pl.ds(0, DESTS - 1)]
        pltpu.make_async_copy(sent, sent, pack_send).wait()

    pltpu.make_async_copy(out_ref, out_ref, out_sem).wait()


def zonal_sums(grid, waves):
    _, _, _, lo, _ = place()
    rows, lat_local, lon_local = grid.shape
    lon = lon_local * Y
    share = -(-rows // (Y * ROWS)) * ROWS
    steps = share // ROWS
    columns = 2 * waves.size
    fine = 32
    waves = jnp.broadcast_to(waves[:, :, None, :], waves.shape[:2] + (2, PLANE))
    sine = jnp.broadcast_to(jnp.arange(2)[None, None, :, None], waves.shape).reshape(1, columns) == 1
    waves = waves.reshape(1, columns)
    grid_lon = lon * ZLO

    def angles(longitudes):
        phases = longitudes[:, None] * waves % grid_lon
        return 2.0 * math.pi / grid_lon * phases.astype(jnp.float32)

    base = angles(lo * lon + fine * jnp.arange(lon // fine, dtype=jnp.int32))
    near = angles(jnp.arange(fine, dtype=jnp.int32))
    scale = math.sqrt(2.0 / grid_lon)
    base_cos, base_sin = jnp.cos(base) * scale, jnp.sin(base) * scale
    u = jnp.where(sine, base_sin, base_cos)
    v = jnp.where(sine, base_cos, -base_sin)
    half = columns // 2
    packed = (lat_local, ROWS * half // DESTS)
    chain = pltpu.VMEM((steps, ROWS * lat_local, half), jnp.bfloat16)
    vmem = pl.BlockSpec(memory_space=pltpu.VMEM)
    hbm = pl.BlockSpec(memory_space=pl.ANY)
    dma = pltpu.SemaphoreType.DMA
    return pl.pallas_call(
        functools.partial(zonal_kernel, rows, share, steps),
        out_shape=jax.ShapeDtypeStruct((steps, ZHI) + packed, jnp.bfloat16),
        in_specs=[hbm, vmem, vmem, vmem, vmem],
        out_specs=hbm,
        scratch_shapes=[
            pltpu.VMEM((share, lat_local, lon), jnp.bfloat16),
            pltpu.VMEM((lon, columns), jnp.bfloat16),
            chain,
            chain,
            chain,
            chain,
            pltpu.VMEM((steps, DESTS) + packed, jnp.bfloat16),
            pltpu.VMEM((ROWS * lat_local, half), jnp.float32),
            dma((steps,)),
            dma,
            dma,
            dma((steps,)),
            dma,
            dma((steps,)),
            dma,
            dma,
        ],
        compiler_params=pltpu.CompilerParams(
            collective_id=0, has_side_effects=True, vmem_limit_bytes=48 << 20
        ),
    )(grid, u, v, jnp.cos(near), jnp.sin(near))


def plane_kernel(in_ref, out_ref, send_sem, recv_sem):
    x, hi, core, lo, y = place()
    mine = (x * CORE + core) * Y + y

    def peer(offset):
        other = (mine + offset) % PLANE
        return other, device(other // (CORE * Y), hi, other // Y % CORE, lo, other % Y)

    barrier = pltpu.get_barrier_semaphore()

    def greet(offset, carry):
        pl.semaphore_signal(barrier, inc=1, device_id=peer(offset)[1], device_id_type=MESH)
        return carry

    lax.fori_loop(1, PLANE, greet, 0)
    pl.semaphore_wait(barrier, PLANE - 1)
    pltpu.make_async_copy(in_ref.at[mine], out_ref.at[mine], recv_sem).start()

    def send(offset, carry):
        other, where = peer(offset)
        pltpu.make_async_remote_copy(
            src_ref=in_ref.at[other],
            dst_ref=out_ref.at[mine],
            send_sem=send_sem,
            recv_sem=recv_sem,
            device_id=where,
            device_id_type=MESH,
        ).start()
        return carry

    lax.fori_loop(1, PLANE, send, 0)
    sent = in_ref.at[pl.ds(0, PLANE - 1)]
    pltpu.make_async_copy(sent, sent, send_sem).wait()
    pltpu.make_async_copy(out_ref, out_ref, recv_sem).wait()


def plane_exchange(blocks):
    hbm = pl.BlockSpec(memory_space=pl.ANY)
    return pl.pallas_call(
        plane_kernel,
        out_shape=jax.ShapeDtypeStruct(blocks.shape, blocks.dtype),
        in_specs=[hbm],
        out_specs=hbm,
        scratch_shapes=[pltpu.SemaphoreType.DMA, pltpu.SemaphoreType.DMA],
        compiler_params=pltpu.CompilerParams(collective_id=1, has_side_effects=True),
    )(blocks)


def meridional_table(grid_lat, lat_local):
    modes = jnp.arange(grid_lat, dtype=jnp.int32)
    owner = jnp.arange(X * ZHI * CORE, dtype=jnp.int32).reshape(X, ZHI, CORE)
    owner = owner.transpose(0, 2, 1).reshape(-1)

    def angles(halves):
        phases = modes[None, :] * halves[:, None] % (4 * grid_lat)
        return math.pi / (2 * grid_lat) * phases.astype(jnp.float32)

    base = angles(2 * lat_local * owner)
    near = angles(2 * jnp.arange(lat_local, dtype=jnp.int32) + 1)
    scale = math.sqrt(2.0 / grid_lat)
    base_cos, base_sin = jnp.cos(base)[:, None] * scale, jnp.sin(base)[:, None] * scale
    table = base_cos * jnp.cos(near)[None] - base_sin * jnp.sin(near)[None]
    return table.reshape(grid_lat, grid_lat).astype(jnp.bfloat16)


def band_apply(blocks, diagonal_blocks, lower_blocks):
    result = jnp.einsum(
        "bij,crbj->crbi", diagonal_blocks, blocks, preferred_element_type=jnp.float32
    )
    below = jnp.einsum(
        "bij,crbj->crbi", lower_blocks, blocks[:, :, :-1], preferred_element_type=jnp.float32
    )
    above = jnp.einsum(
        "bji,crbj->crbi", lower_blocks, blocks[:, :, 1:], preferred_element_type=jnp.float32
    )
    below = jnp.pad(below, ((0, 0), (0, 0), (1, 0), (0, 0)))
    above = jnp.pad(above, ((0, 0), (0, 0), (0, 1), (0, 0)))
    return result + below + above


def per_device(cotangent, wave_order, band_diagonal, band_lower, vertical_matrix):
    fields, levels, lat_local, lon_local = cotangent.shape
    rows = fields * levels
    grid_lat = lat_local * X * ZHI * CORE
    _, hi, _, _, _ = place()
    to_hi = (hi + jnp.array(GROUP_STEP)) % ZHI
    plane = jnp.arange(PLANE)
    slots = (to_hi * CORE * ZLO + jnp.array(GROUP_PLACE))[:, :, None] * Y + (
        (plane // (CORE * Y) * ZHI * CORE + plane // Y % CORE) * ZLO * Y + plane % Y
    )
    coeffs = zonal_sums(cotangent.reshape(rows, lat_local, lon_local), wave_order[slots])
    steps = coeffs.shape[0]
    share = steps * ROWS
    coeffs = coeffs.reshape(steps, ZHI, lat_local, ROWS, 2, PLANE)
    blocks = coeffs.transpose(5, 4, 0, 3, 1, 2).reshape(PLANE, -1, 128)
    gathered = plane_exchange(blocks).reshape(X * CORE, Y, 2, share, ZHI * lat_local)
    gathered = gathered.transpose(2, 1, 3, 0, 4).reshape(2, Y * share, grid_lat)
    spare = Y * share - rows
    gathered = jnp.concatenate(
        [gathered[:, : (Y - 1) * share], gathered[:, (Y - 1) * share + spare :]], axis=1
    )
    spectra = jnp.einsum(
        "crn,nk->crk",
        gathered,
        meridional_table(grid_lat, lat_local),
        preferred_element_type=jnp.float32,
    ).astype(jnp.bfloat16)
    block_count = band_diagonal.shape[1]
    diagonal_blocks = band_diagonal[0].reshape(block_count, BLK, BLK)
    lower_blocks = band_lower[0].reshape(block_count - 1, BLK, BLK)
    blocks = spectra.reshape(2, rows, block_count, BLK)
    banded = band_apply(blocks, diagonal_blocks, lower_blocks).astype(jnp.bfloat16)
    layered = banded.reshape(2, fields, levels, grid_lat)
    mixed = jnp.einsum(
        "flm,cflk->cfmk", vertical_matrix, layered, preferred_element_type=jnp.float32
    )
    return mixed.astype(jnp.bfloat16)[None]


def solution(mesh):
    return jax.shard_map(
        per_device,
        mesh=mesh,
        in_specs=(
            P(None, None, "lat", "lon"),
            P(),
            P(("lat", "lon"), None, None),
            P(("lat", "lon"), None, None),
            P(),
        ),
        out_specs=P(("lat", "lon"), None, None, None, None),
        check_vma=False,
    )
```

```python
import functools
import math

import jax
import jax.numpy as jnp
from jax import lax
from jax.experimental import pallas as pl
from jax.experimental.pallas import tpu as pltpu
from jax.sharding import PartitionSpec as P

BLK = 64
MESH = pl.DeviceIdType.MESH

X, ZHI, CORE, ZLO, Y = 4, 4, 2, 4, 4
PLANE = X * CORE * Y
SIDES, DESTS = 2, 8
GROUP_STEP = ((3, 3, 3, 3, 2, 2, 0, 0), (1, 1, 1, 1, 2, 2, 0, 0))
GROUP_PLACE = ((0, 1, 2, 3, 2, 3, 0, 1), (0, 1, 2, 3, 0, 1, 2, 3))
ROWS = 2
AHEAD = 4
COARSE = 32
SKEW = 2


def place():
    lat, lon = lax.axis_index("lat"), lax.axis_index("lon")
    return lat // (ZHI * CORE), lat // CORE % ZHI, lat % CORE, lon // Y, lon % Y


def device(x, hi, core, lo, y):
    return ((x * ZHI + hi) * CORE + core, lo * Y + y)


def cosine(phase, period):
    quarter = period // 4
    turns = jnp.floor(phase * (1.0 / quarter) + 0.5)
    angle = (phase - turns * quarter) * (2.0 * math.pi / period)
    square = angle * angle
    even = 1.0 + square * (
        -1 / 2 + square * (1 / 24 + square * (-1 / 720 + square * (1 / 40320)))
    )
    odd = angle * (
        1.0 + square * (-1 / 6 + square * (1 / 120 + square * (-1 / 5040 + square * (1 / 362880))))
    )
    turn = turns.astype(jnp.int32) & 3
    value = jnp.where((turn & 1) == 1, odd, even)
    return jnp.where((turn == 1) | (turn == 2), -value, value)


def slots_of_columns(hi, column):
    width = 2 * PLANE
    side, dest, plane = column // (DESTS * width), column // width % DESTS, column % PLANE
    step = jnp.where(dest < 4, jnp.where(side == 0, 3, 1), jnp.where(dest < 6, 2, 0))
    low_side = jnp.where(dest < 4, dest, jnp.where(dest < 6, dest - 2, dest - 6))
    lo = jnp.where(side == 0, low_side, dest % 4)
    lo = jnp.where((side == 1) & (dest >= 6), dest - 4, lo)
    to_hi = (hi + step) % ZHI
    x, core, y = plane // (CORE * Y), plane // Y % CORE, plane % Y
    return (((x * ZHI + to_hi) * CORE + core) * ZLO + lo) * Y + y


def waves_of_columns(wave_ref, hi, columns):
    slots = wave_ref.shape[1]
    slot = slots_of_columns(hi, lax.broadcasted_iota(jnp.int32, (1, columns), 1))
    wave = jnp.broadcast_to(wave_ref[...], (8, slots))
    pick = lax.broadcasted_iota(jnp.int32, (slots, columns), 0) == slot
    pick = jnp.where(pick, 1.0, 0.0).astype(jnp.bfloat16)

    def picked(digits):
        digits = digits.astype(jnp.float32).astype(jnp.bfloat16)
        return jnp.dot(digits, pick, preferred_element_type=jnp.float32)[:1]

    return picked(wave // 16) * 16.0 + picked(wave % 16)


def zonal_kernel(
    rows, share, steps,
    grid_ref, wave_ref, out_ref,
    grid, basis, u_ref, v_ref, right_in, left_in, right_out, left_out, packed, total,
    grid_sem, grid_send, right_send, right_recv, left_send, left_recv,
    pack_send, out_sem,
):
    x, hi, core, lo, y = place()
    lat_local, lon_local = grid_ref.shape[1:]
    half = basis.shape[1] // 2
    width = half // DESTS

    barrier = pltpu.get_barrier_semaphore()
    for step in range(1, Y):
        pl.semaphore_signal(
            barrier, inc=1, device_id=device(x, hi, core, lo, (y + step) % Y), device_id_type=MESH
        )
    for step in range(1, ZHI * ZLO):
        z = (hi * ZLO + lo + step) % (ZHI * ZLO)
        pl.semaphore_signal(
            barrier, inc=1, device_id=device(x, z // ZLO, core, z % ZLO, y), device_id_type=MESH
        )
    pl.semaphore_wait(barrier, Y - 1 + ZHI * ZLO - 1)

    def first_row(owner):
        return jnp.minimum(owner * share, rows - share)

    def grid_copies(step):
        columns = pl.ds(pl.multiple_of(y * lon_local, lon_local), lon_local)
        target = grid.at[pl.ds(step * ROWS, ROWS), :, columns]
        for offset in range(1, Y):
            owner = (y + offset) % Y
            pltpu.make_async_remote_copy(
                src_ref=grid_ref.at[pl.ds(first_row(owner) + step * ROWS, ROWS)],
                dst_ref=target,
                send_sem=grid_send,
                recv_sem=grid_sem.at[step],
                device_id=device(x, hi, core, lo, owner),
                device_id_type=MESH,
            ).start()
        pltpu.make_async_copy(
            grid_ref.at[pl.ds(first_row(y) + step * ROWS, ROWS)], target, grid_sem.at[step]
        ).start()

    for step in range(AHEAD):
        grid_copies(step)

    waves = waves_of_columns(wave_ref, hi, basis.shape[1])
    column = lax.broadcasted_iota(jnp.int32, (1, basis.shape[1]), 1)
    sine = jnp.where(column // PLANE % 2 == 1, 1.0, 0.0)
    lon, grid_lon = basis.shape[0], basis.shape[0] * ZLO
    coarse, fine = u_ref.shape[0], lon // u_ref.shape[0]
    scale = math.sqrt(2.0 / grid_lon)
    first = (lo * lon + fine * lax.broadcasted_iota(jnp.int32, (coarse, 1), 0)).astype(jnp.float32)
    base = waves * first - sine * (grid_lon // 4)
    u_ref[...] = cosine(base, grid_lon) * scale
    v_ref[...] = cosine(base + grid_lon // 4, grid_lon) * scale
    near = waves * lax.broadcasted_iota(jnp.int32, (fine, 1), 0).astype(jnp.float32)
    near_cos, near_sin = cosine(near, grid_lon), cosine(near - grid_lon // 4, grid_lon)

    def fill(a, carry):
        piece = u_ref[pl.ds(a, 1), :] * near_cos + v_ref[pl.ds(a, 1), :] * near_sin
        basis[pl.ds(pl.multiple_of(a * fine, fine), fine), :] = piece.astype(basis.dtype)
        return carry

    lax.fori_loop(0, coarse, fill, 0)

    def product(step, side):
        left = grid[pl.ds(step * ROWS, ROWS)].reshape(ROWS * lat_local, grid.shape[2])
        return jnp.dot(
            left, basis[:, side * half : (side + 1) * half], preferred_element_type=jnp.float32
        )

    def hand_out(step, side):
        for pair in range(DESTS // 2):
            lanes = slice(pair * 2 * width, (pair + 1) * 2 * width)
            top, low = total[:lat_local, lanes], total[lat_local:, lanes]
            for odd in range(2):
                part = slice(odd * width, (odd + 1) * width)
                packed[step, pair * 2 + odd] = jnp.concatenate(
                    [top[:, part], low[:, part]], axis=1
                ).astype(packed.dtype)
        own_lo = ZLO - 1 if side else 0
        for dest in range(DESTS):
            to_hi = (hi + GROUP_STEP[side][dest]) % ZHI
            to_lo = GROUP_PLACE[side][dest]
            if GROUP_STEP[side][dest] == 0 and to_lo == own_lo:
                pltpu.make_async_copy(packed.at[step, dest], out_ref.at[step, hi], out_sem).start()
            else:
                pltpu.make_async_remote_copy(
                    src_ref=packed.at[step, dest],
                    dst_ref=out_ref.at[step, hi],
                    send_sem=pack_send,
                    recv_sem=out_sem,
                    device_id=device(x, to_hi, core, to_lo, y),
                    device_id_type=MESH,
                ).start()

    def chain(step, side):
        arrived, leaving = (right_in, right_out) if side else (left_in, left_out)
        send_sem, recv_sem = (right_send, right_recv) if side else (left_send, left_recv)
        first, last = (0, ZLO - 1) if side else (ZLO - 1, 0)
        total[...] = product(step, side)

        @pl.when(lo != first)
        def _():
            pltpu.make_async_copy(arrived.at[step], arrived.at[step], recv_sem.at[step]).wait()
            total[...] += arrived[step].astype(jnp.float32)

        @pl.when(lo != last)
        def _():
            leaving[step] = total[...].astype(leaving.dtype)
            pltpu.make_async_remote_copy(
                src_ref=leaving.at[step],
                dst_ref=arrived.at[step],
                send_sem=send_sem,
                recv_sem=recv_sem.at[step],
                device_id=device(x, hi, core, lo + (1 if side else -1), y),
                device_id_type=MESH,
            ).start()

        @pl.when(lo == last)
        def _():
            hand_out(step, side)

    def one(step, carry):
        @pl.when(step + AHEAD < steps)
        def _():
            grid_copies(step + AHEAD)

        first = step - SKEW * jnp.minimum(lo, ZLO - 1 - lo)

        @pl.when((first >= 0) & (first < steps))
        def _():
            block = grid.at[pl.ds(first * ROWS, ROWS)]
            pltpu.make_async_copy(block, block, grid_sem.at[first]).wait()

        for side in range(SIDES):
            at = step - SKEW * (lo if side else ZLO - 1 - lo)

            @pl.when((at >= 0) & (at < steps))
            def _():
                chain(at, side)

        return carry

    lax.fori_loop(0, steps + SKEW * (ZLO - 1), one, 0)

    sent = grid_ref.at[pl.ds(0, (Y - 1) * share)]
    pltpu.make_async_copy(sent, sent, grid_send).wait()

    @pl.when(lo != ZLO - 1)
    def _():
        pltpu.make_async_copy(right_out, right_out, right_send).wait()

    @pl.when(lo != 0)
    def _():
        pltpu.make_async_copy(left_out, left_out, left_send).wait()

    @pl.when((lo == 0) | (lo == ZLO - 1))
    def _():
        sent = packed.at[:, pl.ds(0, DESTS - 1)]
        pltpu.make_async_copy(sent, sent, pack_send).wait()

    pltpu.make_async_copy(out_ref, out_ref, out_sem).wait()


def zonal_sums(grid, wave_order):
    rows, lat_local, lon_local = grid.shape
    lon = lon_local * Y
    share = -(-rows // (Y * ROWS)) * ROWS
    steps = share // ROWS
    columns = 2 * wave_order.size
    half = columns // 2
    packed = (lat_local, ROWS * half // DESTS)
    chain = pltpu.VMEM((steps, ROWS * lat_local, half), jnp.bfloat16)
    hbm = pl.BlockSpec(memory_space=pl.ANY)
    dma = pltpu.SemaphoreType.DMA
    return pl.pallas_call(
        functools.partial(zonal_kernel, rows, share, steps),
        out_shape=jax.ShapeDtypeStruct((steps, ZHI) + packed, jnp.bfloat16),
        in_specs=[hbm, pl.BlockSpec(memory_space=pltpu.VMEM)],
        out_specs=hbm,
        scratch_shapes=[
            pltpu.VMEM((share, lat_local, lon), jnp.bfloat16),
            pltpu.VMEM((lon, columns), jnp.bfloat16),
            pltpu.VMEM((COARSE, columns), jnp.float32),
            pltpu.VMEM((COARSE, columns), jnp.float32),
            chain,
            chain,
            chain,
            chain,
            pltpu.VMEM((steps, DESTS) + packed, jnp.bfloat16),
            pltpu.VMEM((ROWS * lat_local, half), jnp.float32),
            dma((steps,)),
            dma,
            dma,
            dma((steps,)),
            dma,
            dma((steps,)),
            dma,
            dma,
        ],
        compiler_params=pltpu.CompilerParams(
            collective_id=0, has_side_effects=True, vmem_limit_bytes=61 << 20
        ),
    )(grid, wave_order.reshape(1, -1))


def mode_kernel(
    rows, share,
    in_ref, diagonal_ref, lower_ref, vertical_ref, out_ref,
    wide, spread, sending, gathered, table, base_cos, base_sin,
    diagonal, lower, band, levels_pad, mix, spectra, banded, total,
    send_sem, recv_sem,
):
    x, hi, core, lo, y = place()
    mine = (x * CORE + core) * Y + y
    steps, _, lat_local, _ = in_ref.shape
    span = ZHI * lat_local
    depth = sending.shape[1]
    fields, levels = vertical_ref.shape[:2]
    grid_lat = table.shape[1]
    blocks = diagonal_ref.shape[0]
    f32, bf16 = jnp.float32, jnp.bfloat16

    def peer(offset):
        other = (mine + offset) % PLANE
        return other, device(other // (CORE * Y), hi, other // Y % CORE, lo, other % Y)

    barrier = pltpu.get_barrier_semaphore()

    def greet(offset, carry):
        pl.semaphore_signal(barrier, inc=1, device_id=peer(offset)[1], device_id_type=MESH)
        return carry

    lax.fori_loop(1, PLANE, greet, 0)

    wide[...] = jnp.zeros_like(wide)
    for row in range(4 * steps, depth):
        for part in range(2):
            spread[part, pl.ds(row, PLANE, stride=depth), :] = jnp.zeros((PLANE, 128), f32)

    def turn(step, carry):
        wide[:span, :] = in_ref[step].reshape(span, 128).astype(f32)
        turned = wide[...].T
        for group in range(4):
            for part in range(2):
                spread[part, pl.ds(4 * step + group, PLANE, stride=depth), :] = turned[
                    group * PLANE : (group + 1) * PLANE, part * 128 : (part + 1) * 128
                ]
        return carry

    lax.fori_loop(0, steps, turn, 0)

    def narrow(other, carry):
        at = pl.ds(pl.multiple_of(other * depth, depth), depth)
        for part in range(2):
            sending[other, :, part * 128 : (part + 1) * 128] = spread[part, at, :].astype(bf16)
        return carry

    lax.fori_loop(0, PLANE, narrow, 0)

    pl.semaphore_wait(barrier, PLANE - 1)

    def send(offset, carry):
        other, where = peer(offset)
        pltpu.make_async_remote_copy(
            src_ref=sending.at[other],
            dst_ref=gathered.at[mine],
            send_sem=send_sem,
            recv_sem=recv_sem,
            device_id=where,
            device_id_type=MESH,
        ).start()
        return carry

    lax.fori_loop(1, PLANE, send, 0)
    pltpu.make_async_copy(sending.at[mine], gathered.at[mine], recv_sem).start()

    scale = math.sqrt(2.0 / grid_lat)
    mode = lax.broadcasted_iota(jnp.int32, (1, grid_lat), 1).astype(f32)
    owners = X * ZHI * CORE
    base = 2 * lat_local * lax.broadcasted_iota(jnp.int32, (owners, 1), 0)
    base = base.astype(f32) * mode
    base_cos[...] = cosine(base, 4 * grid_lat) * scale
    base_sin[...] = cosine(base - grid_lat, 4 * grid_lat) * scale
    near = (2 * lax.broadcasted_iota(jnp.int32, (lat_local, 1), 0) + 1).astype(f32) * mode
    near_cos, near_sin = cosine(near, 4 * grid_lat), cosine(near - grid_lat, 4 * grid_lat)

    def fill(owner, carry):
        to_x, to_hi, to_core = owner // (ZHI * CORE), owner // CORE % ZHI, owner % CORE
        at = (to_x * CORE + to_core) * 256 + to_hi * lat_local
        piece = base_cos[pl.ds(owner, 1), :] * near_cos - base_sin[pl.ds(owner, 1), :] * near_sin
        table[pl.ds(pl.multiple_of(at, 16), lat_local), :] = piece.astype(bf16)
        return carry

    lax.fori_loop(0, owners, fill, 0)
    for source in range(X * CORE):
        table[source * 256 + span : (source + 1) * 256, :] = jnp.zeros((256 - span, grid_lat), bf16)

    for row in range(BLK):
        tile = slice(row // 2 * 128, row // 2 * 128 + 128)
        for flat, square in ((diagonal_ref, diagonal), (lower_ref, lower)):
            piece = flat[:, tile].astype(f32)
            if row % 2:
                piece = pltpu.roll(piece, 64, 1)
            square[pl.ds(row, flat.shape[0], stride=BLK), :] = piece

    empty = jnp.zeros((BLK, BLK), f32)

    def square(ref, block):
        return ref[block * BLK : (block + 1) * BLK, :BLK]

    for pair in range(blocks // 2):
        one, two = 2 * pair, 2 * pair + 1
        before = square(lower, one - 1) if pair else empty
        after = square(lower, two).T if two < blocks - 1 else empty
        inner = square(lower, one)
        top = (empty, before, square(diagonal, one), inner.T, empty, empty)
        low = (empty, empty, inner, square(diagonal, two), after, empty)
        band[pair, :BLK, :] = jnp.concatenate(top, axis=1).astype(bf16)
        band[pair, BLK:, :] = jnp.concatenate(low, axis=1).astype(bf16)

    held = mix.shape[1]
    at = lax.broadcasted_iota(jnp.int32, (1, held), 1)
    owner, within = at // depth, at % depth
    start = jnp.minimum(owner * share, rows - share)
    row = start + within // 2
    fresh = (row >= owner * share) & (within < 2 * share)
    level = lax.broadcasted_iota(jnp.int32, (BLK, 1), 0)
    for field in range(fields):
        levels_pad[...] = jnp.zeros_like(levels_pad)
        levels_pad[:levels, :levels] = vertical_ref[field].astype(f32)
        turned = levels_pad[...].T[:BLK, :].astype(bf16)
        pick = (row == field * levels + level) & (level < levels) & fresh
        pick = jnp.where(pick, 1.0, 0.0).astype(bf16)
        pick = jnp.concatenate([pick, jnp.zeros((128 - BLK, held), bf16)], axis=0)
        mixed = jnp.dot(turned, pick, preferred_element_type=f32)
        for c in range(2):
            part = c * fields + field
            mix[part * BLK : (part + 1) * BLK, :] = jnp.where(at % 2 == c, mixed, 0.0).astype(bf16)

    sent = sending.at[pl.ds(0, PLANE - 1)]
    pltpu.make_async_copy(sent, sent, send_sem).wait()
    pltpu.make_async_copy(gathered, gathered, recv_sem).wait()

    width = total.shape[1]
    for tile in range(grid_lat // width):
        lanes = slice(tile * width, (tile + 1) * width)
        for source in range(X * CORE):
            left = gathered[source * Y : (source + 1) * Y].reshape(held, 256)
            term = jnp.dot(
                left, table[source * 256 : (source + 1) * 256, lanes], preferred_element_type=f32
            )
            if source == 0:
                total[...] = term
            else:
                total[...] += term
        spectra[:, lanes] = total[...].astype(bf16)

    for pair in range(blocks // 2):
        begin, end = max(0, pair - 1) * 128, min(blocks // 2, pair + 2) * 128
        skip = 0 if pair else 128
        banded[:, pair * 128 : (pair + 1) * 128] = lax.dot_general(
            spectra[:, begin:end],
            band[pair, :, skip : skip + end - begin],
            (((1,), (1,)), ((), ())),
            preferred_element_type=f32,
        ).astype(bf16)

    for tile in range(grid_lat // width):
        lanes = slice(tile * width, (tile + 1) * width)
        result = jnp.dot(mix[...], banded[:, lanes], preferred_element_type=f32)
        for c in range(2):
            for field in range(fields):
                at = (c * fields + field) * BLK
                out_ref[c, field, :, lanes] = result[at : at + levels].astype(out_ref.dtype)


def finish(coeffs, diagonal, lower, vertical, rows, grid_lat):
    fields, levels = vertical.shape[:2]
    steps = coeffs.shape[0]
    share = steps * ROWS
    depth = -(-2 * share // 16) * 16
    blocks = diagonal.shape[0]
    vmem = pl.BlockSpec(memory_space=pltpu.VMEM)
    f32, bf16 = jnp.float32, jnp.bfloat16
    return pl.pallas_call(
        functools.partial(mode_kernel, rows, share),
        out_shape=jax.ShapeDtypeStruct((2, fields, levels, grid_lat), bf16),
        in_specs=[vmem] * 4,
        out_specs=vmem,
        scratch_shapes=[
            pltpu.VMEM((256, 128), f32),
            pltpu.VMEM((2, PLANE * depth, 128), f32),
            pltpu.VMEM((PLANE, depth, 256), bf16),
            pltpu.VMEM((PLANE, depth, 256), bf16),
            pltpu.VMEM((X * CORE * 256, grid_lat), bf16),
            pltpu.VMEM((X * ZHI * CORE, grid_lat), f32),
            pltpu.VMEM((X * ZHI * CORE, grid_lat), f32),
            pltpu.VMEM((blocks * BLK, 128), f32),
            pltpu.VMEM(((blocks - 1) * BLK, 128), f32),
            pltpu.VMEM((blocks // 2, 2 * BLK, 6 * BLK), bf16),
            pltpu.VMEM((128, 128), f32),
            pltpu.VMEM((2 * fields * BLK, Y * depth), bf16),
            pltpu.VMEM((Y * depth, grid_lat), bf16),
            pltpu.VMEM((Y * depth, grid_lat), bf16),
            pltpu.VMEM((Y * depth, 512), f32),
            pltpu.SemaphoreType.DMA,
            pltpu.SemaphoreType.DMA,
        ],
        compiler_params=pltpu.CompilerParams(
            collective_id=1, has_side_effects=True, vmem_limit_bytes=48 << 20
        ),
    )(coeffs, diagonal, lower, vertical)


def per_device(cotangent, wave_order, band_diagonal, band_lower, vertical_matrix):
    fields, levels, lat_local, lon_local = cotangent.shape
    rows = fields * levels
    coeffs = zonal_sums(cotangent.reshape(rows, lat_local, lon_local), wave_order)
    return finish(
        coeffs, band_diagonal[0], band_lower[0], vertical_matrix, rows, lat_local * X * ZHI * CORE
    )[None]


def solution(mesh):
    return jax.shard_map(
        per_device,
        mesh=mesh,
        in_specs=(
            P(None, None, "lat", "lon"),
            P(),
            P(("lat", "lon"), None, None),
            P(("lat", "lon"), None, None),
            P(),
        ),
        out_specs=P(("lat", "lon"), None, None, None, None),
        check_vma=False,
    )
```

```python
import functools
import math

import jax
import jax.numpy as jnp
from jax import lax
from jax.experimental import pallas as pl
from jax.experimental.pallas import tpu as pltpu
from jax.sharding import PartitionSpec as P

BLK = 64
MESH = pl.DeviceIdType.MESH

X, ZHI, CORE, ZLO, Y = 4, 4, 2, 4, 4
PLANE = X * CORE * Y
GROUP = 4
SIDES, DESTS = 2, 8
GROUP_STEP = ((3, 3, 3, 3, 2, 2, 0, 0), (1, 1, 1, 1, 2, 2, 0, 0))
GROUP_PLACE = ((0, 1, 2, 3, 2, 3, 0, 1), (0, 1, 2, 3, 0, 1, 2, 3))
ROWS = 2
AHEAD = 4
LAG = 3
COARSE = 32
SKEW = 2


def place():
    lat, lon = lax.axis_index("lat"), lax.axis_index("lon")
    return lat // (ZHI * CORE), lat // CORE % ZHI, lat % CORE, lon // Y, lon % Y


def device(x, hi, core, lo, y):
    return ((x * ZHI + hi) * CORE + core, lo * Y + y)


def cosine(phase, period):
    quarter = period // 4
    turns = jnp.floor(phase * (1.0 / quarter) + 0.5)
    angle = (phase - turns * quarter) * (2.0 * math.pi / period)
    square = angle * angle
    even = 1.0 + square * (
        -1 / 2 + square * (1 / 24 + square * (-1 / 720 + square * (1 / 40320)))
    )
    odd = angle * (
        1.0 + square * (-1 / 6 + square * (1 / 120 + square * (-1 / 5040 + square * (1 / 362880))))
    )
    turn = turns.astype(jnp.int32) & 3
    value = jnp.where((turn & 1) == 1, odd, even)
    return jnp.where((turn == 1) | (turn == 2), -value, value)


def slots_of_columns(hi, column):
    width = 2 * PLANE
    side, dest, plane = column // (DESTS * width), column // width % DESTS, column % PLANE
    step = jnp.where(dest < 4, jnp.where(side == 0, 3, 1), jnp.where(dest < 6, 2, 0))
    low_side = jnp.where(dest < 4, dest, jnp.where(dest < 6, dest - 2, dest - 6))
    lo = jnp.where(side == 0, low_side, dest % 4)
    lo = jnp.where((side == 1) & (dest >= 6), dest - 4, lo)
    to_hi = (hi + step) % ZHI
    x, core, y = plane // (CORE * Y), plane // Y % CORE, plane % Y
    return (((x * ZHI + to_hi) * CORE + core) * ZLO + lo) * Y + y


def waves_of_columns(wave_ref, hi, columns):
    slots = wave_ref.shape[1]
    slot = slots_of_columns(hi, lax.broadcasted_iota(jnp.int32, (1, columns), 1))
    wave = jnp.broadcast_to(wave_ref[...], (8, slots))
    pick = lax.broadcasted_iota(jnp.int32, (slots, columns), 0) == slot
    pick = jnp.where(pick, 1.0, 0.0).astype(jnp.bfloat16)

    def picked(digits):
        digits = digits.astype(jnp.float32).astype(jnp.bfloat16)
        return jnp.dot(digits, pick, preferred_element_type=jnp.float32)[:1]

    return picked(wave // 16) * 16.0 + picked(wave % 16)


def step_kernel(
    rows, share, steps,
    grid_ref, wave_ref, diagonal_ref, lower_ref, vertical_ref, out_ref,
    grid, basis, u_ref, v_ref, right_in, left_in, right_out, left_out, packed, total,
    parts, wide, spread, sending, gathered,
    table, base_cos, base_sin, near_cos, near_sin,
    diagonal, lower, band, levels_pad, mix, spectra, banded,
    grid_sem, grid_send, right_send, right_recv, left_send, left_recv,
    pack_send, part_sem, plane_send, plane_sem,
):
    x, hi, core, lo, y = place()
    mine = (x * CORE + core) * Y + y
    lat_local, lon_local = grid_ref.shape[1:]
    half = basis.shape[1] // 2
    width = half // DESTS
    f32, bf16 = jnp.float32, jnp.bfloat16

    def peer(offset):
        other = (mine + offset) % PLANE
        return other, device(other // (CORE * Y), hi, other // Y % CORE, lo, other % Y)

    barrier = pltpu.get_barrier_semaphore()

    def greet_line(offset, carry):
        z = (hi * ZLO + lo + offset) % (ZHI * ZLO)
        pl.semaphore_signal(
            barrier, inc=1, device_id=device(x, z // ZLO, core, z % ZLO, y), device_id_type=MESH
        )
        return carry

    def greet_plane(offset, carry):
        pl.semaphore_signal(barrier, inc=1, device_id=peer(offset)[1], device_id_type=MESH)
        return carry

    lax.fori_loop(1, ZHI * ZLO, greet_line, 0)
    lax.fori_loop(1, PLANE, greet_plane, 0)
    pl.semaphore_wait(barrier, ZHI * ZLO - 1 + PLANE - 1)

    def first_row(owner):
        return jnp.minimum(owner * share, rows - share)

    def grid_copies(step):
        columns = pl.ds(pl.multiple_of(y * lon_local, lon_local), lon_local)
        target = grid.at[pl.ds(step * ROWS, ROWS), :, columns]
        for offset in range(1, Y):
            owner = (y + offset) % Y
            pltpu.make_async_remote_copy(
                src_ref=grid_ref.at[pl.ds(first_row(owner) + step * ROWS, ROWS)],
                dst_ref=target,
                send_sem=grid_send,
                recv_sem=grid_sem.at[step],
                device_id=device(x, hi, core, lo, owner),
                device_id_type=MESH,
            ).start()
        pltpu.make_async_copy(
            grid_ref.at[pl.ds(first_row(y) + step * ROWS, ROWS)], target, grid_sem.at[step]
        ).start()

    for step in range(AHEAD):
        grid_copies(step)

    waves = waves_of_columns(wave_ref, hi, basis.shape[1])
    column = lax.broadcasted_iota(jnp.int32, (1, basis.shape[1]), 1)
    sine = jnp.where(column // PLANE % 2 == 1, 1.0, 0.0)
    lon, grid_lon = basis.shape[0], basis.shape[0] * ZLO
    coarse, fine = u_ref.shape[0], lon // u_ref.shape[0]
    scale = math.sqrt(2.0 / grid_lon)
    first = (lo * lon + fine * lax.broadcasted_iota(jnp.int32, (coarse, 1), 0)).astype(f32)
    base = waves * first - sine * (grid_lon // 4)
    u_ref[...] = cosine(base, grid_lon) * scale
    v_ref[...] = cosine(base + grid_lon // 4, grid_lon) * scale
    near = waves * lax.broadcasted_iota(jnp.int32, (fine, 1), 0).astype(f32)
    fine_cos, fine_sin = cosine(near, grid_lon), cosine(near - grid_lon // 4, grid_lon)

    def fill(a, carry):
        piece = u_ref[pl.ds(a, 1), :] * fine_cos + v_ref[pl.ds(a, 1), :] * fine_sin
        basis[pl.ds(pl.multiple_of(a * fine, fine), fine), :] = piece.astype(bf16)
        return carry

    lax.fori_loop(0, coarse, fill, 0)

    def product(step, side):
        left = grid[pl.ds(step * ROWS, ROWS)].reshape(ROWS * lat_local, grid.shape[2])
        return jnp.dot(
            left, basis[:, side * half : (side + 1) * half], preferred_element_type=f32
        )

    def hand_out(step, side):
        for pair in range(DESTS // 2):
            lanes = slice(pair * 2 * width, (pair + 1) * 2 * width)
            top, low = total[:lat_local, lanes], total[lat_local:, lanes]
            for odd in range(2):
                part = slice(odd * width, (odd + 1) * width)
                packed[step, pair * 2 + odd] = jnp.concatenate(
                    [top[:, part], low[:, part]], axis=1
                ).astype(bf16)
        own_lo = ZLO - 1 if side else 0
        for dest in range(DESTS):
            to_hi = (hi + GROUP_STEP[side][dest]) % ZHI
            to_lo = GROUP_PLACE[side][dest]
            if GROUP_STEP[side][dest] == 0 and to_lo == own_lo:
                pltpu.make_async_copy(
                    packed.at[step, dest], parts.at[step, hi], part_sem.at[step]
                ).start()
            else:
                pltpu.make_async_remote_copy(
                    src_ref=packed.at[step, dest],
                    dst_ref=parts.at[step, hi],
                    send_sem=pack_send,
                    recv_sem=part_sem.at[step],
                    device_id=device(x, to_hi, core, to_lo, y),
                    device_id_type=MESH,
                ).start()

    def chain(step, side):
        arrived, leaving = (right_in, right_out) if side else (left_in, left_out)
        send_sem, recv_sem = (right_send, right_recv) if side else (left_send, left_recv)
        first, last = (0, ZLO - 1) if side else (ZLO - 1, 0)
        total[...] = product(step, side)

        @pl.when(lo != first)
        def _():
            pltpu.make_async_copy(arrived.at[step], arrived.at[step], recv_sem.at[step]).wait()
            total[...] += arrived[step].astype(f32)

        @pl.when(lo != last)
        def _():
            leaving[step] = total[...].astype(bf16)
            pltpu.make_async_remote_copy(
                src_ref=leaving.at[step],
                dst_ref=arrived.at[step],
                send_sem=send_sem,
                recv_sem=recv_sem.at[step],
                device_id=device(x, hi, core, lo + (1 if side else -1), y),
                device_id_type=MESH,
            ).start()

        @pl.when(lo == last)
        def _():
            hand_out(step, side)

    span = ZHI * lat_local
    depth = sending.shape[1]
    tall = 4 * GROUP

    def turn(step):
        pltpu.make_async_copy(parts.at[step], parts.at[step], part_sem.at[step]).wait()
        wide[:span, :] = parts[step].reshape(span, 128).astype(f32)
        turned = wide[...].T
        for group in range(4):
            for part in range(2):
                spread[part, pl.ds(4 * step + group, PLANE, stride=depth), :] = turned[
                    group * PLANE : (group + 1) * PLANE, part * 128 : (part + 1) * 128
                ]

    def through_plane(group):
        at = pl.ds(pl.multiple_of(group * tall, tall), tall)

        def narrow(other, carry):
            begin = pl.multiple_of(other * depth + group * tall, tall)
            for part in range(2):
                sending[other, at, part * 128 : (part + 1) * 128] = spread[
                    part, pl.ds(begin, tall), :
                ].astype(bf16)
            return carry

        lax.fori_loop(0, PLANE, narrow, 0)

        def send(offset, carry):
            other, where = peer(offset)
            pltpu.make_async_remote_copy(
                src_ref=sending.at[other, at],
                dst_ref=gathered.at[mine, at],
                send_sem=plane_send,
                recv_sem=plane_sem.at[group],
                device_id=where,
                device_id_type=MESH,
            ).start()
            return carry

        lax.fori_loop(1, PLANE, send, 0)
        pltpu.make_async_copy(
            sending.at[mine, at], gathered.at[mine, at], plane_sem.at[group]
        ).start()

    grid_lat = table.shape[1]
    blocks = diagonal_ref.shape[0]
    fields, levels = vertical_ref.shape[:2]
    owners = X * ZHI * CORE
    pairs = blocks // 2

    def start_meridional():
        scale = math.sqrt(2.0 / grid_lat)
        mode = lax.broadcasted_iota(jnp.int32, (1, grid_lat), 1).astype(f32)
        base = 2 * lat_local * lax.broadcasted_iota(jnp.int32, (owners, 1), 0)
        base = base.astype(f32) * mode
        base_cos[...] = cosine(base, 4 * grid_lat) * scale
        base_sin[...] = cosine(base - grid_lat, 4 * grid_lat) * scale
        near = (2 * lax.broadcasted_iota(jnp.int32, (lat_local, 1), 0) + 1).astype(f32) * mode
        near_cos[...] = cosine(near, 4 * grid_lat)
        near_sin[...] = cosine(near - grid_lat, 4 * grid_lat)
        wide[...] = jnp.zeros_like(wide)
        for row in range(4 * steps, depth):
            for part in range(2):
                spread[part, pl.ds(row, PLANE, stride=depth), :] = jnp.zeros((PLANE, 128), f32)
        for source in range(X * CORE):
            table[source * 256 + span : (source + 1) * 256, :] = jnp.zeros(
                (256 - span, grid_lat), bf16
            )

    def meridional(owner):
        to_x, to_hi, to_core = owner // (ZHI * CORE), owner // CORE % ZHI, owner % CORE
        at = (to_x * CORE + to_core) * 256 + to_hi * lat_local
        piece = base_cos[pl.ds(owner, 1), :] * near_cos[...]
        piece -= base_sin[pl.ds(owner, 1), :] * near_sin[...]
        table[pl.ds(pl.multiple_of(at, 16), lat_local), :] = piece.astype(bf16)

    def squares(lanes):
        tile = pl.ds(pl.multiple_of(lanes * 128, 128), 128)
        for flat, square in ((diagonal_ref, diagonal), (lower_ref, lower)):
            piece = flat[:, tile].astype(f32)
            square[pl.ds(2 * lanes, flat.shape[0], stride=BLK), :] = piece
            square[pl.ds(2 * lanes + 1, flat.shape[0], stride=BLK), :] = pltpu.roll(piece, 64, 1)

    def square(ref, block):
        return ref[pl.ds(pl.multiple_of(block * BLK, BLK), BLK), :][:, :BLK]

    def band_pair(pair):
        one, two = 2 * pair, 2 * pair + 1
        empty = jnp.zeros((BLK, BLK), f32)
        before = jnp.where(pair > 0, square(lower, jnp.maximum(one - 1, 0)), 0.0)
        after = square(lower, jnp.minimum(two, blocks - 2)).T
        after = jnp.where(two < blocks - 1, after, 0.0)
        inner = square(lower, one)
        top = (empty, before, square(diagonal, one), inner.T, empty, empty)
        low = (empty, empty, inner, square(diagonal, two), after, empty)
        band[pair, :BLK, :] = jnp.concatenate(top, axis=1).astype(bf16)
        band[pair, BLK:, :] = jnp.concatenate(low, axis=1).astype(bf16)

    held = mix.shape[1]

    def mixing():
        at = lax.broadcasted_iota(jnp.int32, (1, held), 1)
        owner, within = at // depth, at % depth
        row = jnp.minimum(owner * share, rows - share) + within // 2
        fresh = (row >= owner * share) & (within < 2 * share)
        level = lax.broadcasted_iota(jnp.int32, (BLK, 1), 0)
        for field in range(fields):
            levels_pad[...] = jnp.zeros_like(levels_pad)
            levels_pad[:levels, :levels] = vertical_ref[field].astype(f32)
            turned = levels_pad[...].T[:BLK, :].astype(bf16)
            pick = (row == field * levels + level) & (level < levels) & fresh
            pick = jnp.where(pick, 1.0, 0.0).astype(bf16)
            pick = jnp.concatenate([pick, jnp.zeros((128 - BLK, held), bf16)], axis=0)
            mixed = jnp.dot(turned, pick, preferred_element_type=f32)
            for c in range(2):
                part = (c * fields + field) * BLK
                mix[part : part + BLK, :] = jnp.where(at % 2 == c, mixed, 0.0).astype(bf16)

    count = steps + SKEW * (ZLO - 1) + LAG
    duties = (
        (start_meridional, 1, 1, 0),
        (mixing, 2, 1, 0),
        (squares, 3, BLK // 2, 2),
        (meridional, 2, owners, 2),
        (band_pair, 3 + BLK // 4, pairs, 2),
    )

    def one(step, carry):
        @pl.when(step + AHEAD < steps)
        def _():
            grid_copies(step + AHEAD)

        first = step - SKEW * jnp.minimum(lo, ZLO - 1 - lo)

        @pl.when((first >= 0) & (first < steps))
        def _():
            block = grid.at[pl.ds(first * ROWS, ROWS)]
            pltpu.make_async_copy(block, block, grid_sem.at[first]).wait()

        for side in range(SIDES):
            at = step - SKEW * (lo if side else ZLO - 1 - lo)

            @pl.when((at >= 0) & (at < steps))
            def _():
                chain(at, side)

        done = step - SKEW * (ZLO - 1) - LAG

        @pl.when(done >= 0)
        def _():
            turn(done)

        @pl.when((done >= 0) & ((done % GROUP == GROUP - 1) | (done == steps - 1)))
        def _():
            through_plane(done // GROUP)

        for duty, begin, number, each in duties:
            if each:

                @pl.when((step >= begin) & (step < begin + number // each))
                def _():
                    for extra in range(each):
                        duty((step - begin) * each + extra)
            else:

                @pl.when(step == begin)
                def _():
                    duty()

        return carry

    lax.fori_loop(0, count, one, 0)

    sent = grid_ref.at[pl.ds(0, (Y - 1) * share)]
    pltpu.make_async_copy(sent, sent, grid_send).wait()

    @pl.when(lo != ZLO - 1)
    def _():
        pltpu.make_async_copy(right_out, right_out, right_send).wait()

    @pl.when(lo != 0)
    def _():
        pltpu.make_async_copy(left_out, left_out, left_send).wait()

    @pl.when((lo == 0) | (lo == ZLO - 1))
    def _():
        sent = packed.at[:, pl.ds(0, DESTS - 1)]
        pltpu.make_async_copy(sent, sent, pack_send).wait()

    groups = depth // tall
    for begin, end in ((0, groups - 1), (groups - 1, groups)):
        for group in range(begin, end):
            block = gathered.at[:, pl.ds(group * tall, tall)]
            pltpu.make_async_copy(block, block, plane_sem.at[group]).wait()
        at = slice(begin * tall, end * tall)
        high = Y * (end - begin) * tall
        left = jnp.concatenate(
            [
                gathered[source * Y : (source + 1) * Y, at].reshape(high, 256)
                for source in range(X * CORE)
            ],
            axis=1,
        )
        for tile in range(grid_lat // 512):
            lanes = slice(tile * 512, (tile + 1) * 512)
            term = jnp.dot(left, table[:, lanes], preferred_element_type=f32)
            spectra[:, at, lanes] = term.astype(bf16).reshape(Y, (end - begin) * tall, 512)
        for pair in range(pairs):
            low, top = max(0, pair - 1) * 128, min(pairs, pair + 2) * 128
            skip = 0 if pair else 128
            banded[:, at, pair * 128 : (pair + 1) * 128] = (
                lax.dot_general(
                    spectra[:, at, low:top].reshape(high, top - low),
                    band[pair, :, skip : skip + top - low],
                    (((1,), (1,)), ((), ())),
                    preferred_element_type=f32,
                )
                .astype(bf16)
                .reshape(Y, (end - begin) * tall, 128)
            )

    sent = sending.at[pl.ds(0, PLANE - 1)]
    pltpu.make_async_copy(sent, sent, plane_send).wait()

    for tile in range(grid_lat // 512):
        lanes = slice(tile * 512, (tile + 1) * 512)
        result = jnp.dot(
            mix[...], banded[:, :, lanes].reshape(held, 512), preferred_element_type=f32
        )
        for c in range(2):
            for field in range(fields):
                at = (c * fields + field) * BLK
                out_ref[c, field, :, lanes] = result[at : at + levels].astype(out_ref.dtype)


def per_device(cotangent, wave_order, band_diagonal, band_lower, vertical_matrix):
    fields, levels, lat_local, lon_local = cotangent.shape
    rows = fields * levels
    grid_lat = lat_local * X * ZHI * CORE
    lon = lon_local * Y
    share = -(-rows // (Y * ROWS)) * ROWS
    steps = share // ROWS
    columns = 2 * wave_order.size
    half = columns // 2
    packed = (lat_local, ROWS * half // DESTS)
    tall = 4 * GROUP
    depth = -(-2 * share // tall) * tall
    owners = X * ZHI * CORE
    blocks = band_diagonal.shape[1]
    f32, bf16 = jnp.float32, jnp.bfloat16
    chain = pltpu.VMEM((steps, ROWS * lat_local, half), bf16)
    hbm = pl.BlockSpec(memory_space=pl.ANY)
    vmem = pl.BlockSpec(memory_space=pltpu.VMEM)
    dma = pltpu.SemaphoreType.DMA
    return pl.pallas_call(
        functools.partial(step_kernel, rows, share, steps),
        out_shape=jax.ShapeDtypeStruct((2, fields, levels, grid_lat), bf16),
        in_specs=[hbm] + [vmem] * 4,
        out_specs=vmem,
        scratch_shapes=[
            pltpu.VMEM((share, lat_local, lon), bf16),
            pltpu.VMEM((lon, columns), bf16),
            pltpu.VMEM((COARSE, columns), f32),
            pltpu.VMEM((COARSE, columns), f32),
            chain,
            chain,
            chain,
            chain,
            pltpu.VMEM((steps, DESTS) + packed, bf16),
            pltpu.VMEM((ROWS * lat_local, half), f32),
            pltpu.VMEM((steps, ZHI) + packed, bf16),
            pltpu.VMEM((256, 128), f32),
            pltpu.VMEM((2, PLANE * depth, 128), f32),
            pltpu.VMEM((PLANE, depth, 256), bf16),
            pltpu.VMEM((PLANE, depth, 256), bf16),
            pltpu.VMEM((X * CORE * 256, grid_lat), bf16),
            pltpu.VMEM((owners, grid_lat), f32),
            pltpu.VMEM((owners, grid_lat), f32),
            pltpu.VMEM((lat_local, grid_lat), f32),
            pltpu.VMEM((lat_local, grid_lat), f32),
            pltpu.VMEM((blocks * BLK, 128), f32),
            pltpu.VMEM(((blocks - 1) * BLK, 128), f32),
            pltpu.VMEM((blocks // 2, 2 * BLK, 6 * BLK), bf16),
            pltpu.VMEM((128, 128), f32),
            pltpu.VMEM((2 * fields * BLK, Y * depth), bf16),
            pltpu.VMEM((Y, depth, grid_lat), bf16),
            pltpu.VMEM((Y, depth, grid_lat), bf16),
            dma((steps,)),
            dma,
            dma,
            dma((steps,)),
            dma,
            dma((steps,)),
            dma,
            dma((steps,)),
            dma,
            dma((depth // tall,)),
        ],
        compiler_params=pltpu.CompilerParams(
            collective_id=0, has_side_effects=True, vmem_limit_bytes=61 << 20
        ),
    )(
        cotangent.reshape(rows, lat_local, lon_local),
        wave_order.reshape(1, -1),
        band_diagonal[0],
        band_lower[0],
        vertical_matrix,
    )[None]


def solution(mesh):
    return jax.shard_map(
        per_device,
        mesh=mesh,
        in_specs=(
            P(None, None, "lat", "lon"),
            P(),
            P(("lat", "lon"), None, None),
            P(("lat", "lon"), None, None),
            P(),
        ),
        out_specs=P(("lat", "lon"), None, None, None, None),
        check_vma=False,
    )
```

```python
import functools
import math

import jax
import jax.numpy as jnp
from jax import lax
from jax.experimental import pallas as pl
from jax.experimental.pallas import tpu as pltpu
from jax.sharding import PartitionSpec as P

BLK = 64
MESH = pl.DeviceIdType.MESH

X, ZHI, CORE, ZLO, Y = 4, 4, 2, 4, 4
PLANE = X * CORE * Y
GROUP = 4
SIDES, DESTS = 2, 8
GROUP_STEP = ((3, 3, 3, 3, 2, 2, 0, 0), (1, 1, 1, 1, 2, 2, 0, 0))
GROUP_PLACE = ((0, 1, 2, 3, 2, 3, 0, 1), (0, 1, 2, 3, 0, 1, 2, 3))
ROWS = 2
FIRST = 2
AHEAD = 2
LAG = 4
COARSE = 32
SKEW = 3


def place():
    lat, lon = lax.axis_index("lat"), lax.axis_index("lon")
    return lat // (ZHI * CORE), lat // CORE % ZHI, lat % CORE, lon // Y, lon % Y


def device(x, hi, core, lo, y):
    return ((x * ZHI + hi) * CORE + core, lo * Y + y)


def cosine(phase, period):
    quarter = period // 4
    turns = jnp.floor(phase * (1.0 / quarter) + 0.5)
    angle = (phase - turns * quarter) * (2.0 * math.pi / period)
    square = angle * angle
    even = 1.0 + square * (
        -1 / 2 + square * (1 / 24 + square * (-1 / 720 + square * (1 / 40320)))
    )
    odd = angle * (
        1.0 + square * (-1 / 6 + square * (1 / 120 + square * (-1 / 5040 + square * (1 / 362880))))
    )
    turn = turns.astype(jnp.int32) & 3
    value = jnp.where((turn & 1) == 1, odd, even)
    return jnp.where((turn == 1) | (turn == 2), -value, value)


def slots_of_columns(hi, column):
    width = 2 * PLANE
    side, dest, plane = column // (DESTS * width), column // width % DESTS, column % PLANE
    step = jnp.where(dest < 4, jnp.where(side == 0, 3, 1), jnp.where(dest < 6, 2, 0))
    low_side = jnp.where(dest < 4, dest, jnp.where(dest < 6, dest - 2, dest - 6))
    lo = jnp.where(side == 0, low_side, dest % 4)
    lo = jnp.where((side == 1) & (dest >= 6), dest - 4, lo)
    to_hi = (hi + step) % ZHI
    x, core, y = plane // (CORE * Y), plane // Y % CORE, plane % Y
    return (((x * ZHI + to_hi) * CORE + core) * ZLO + lo) * Y + y


def waves_of_columns(wave_ref, hi, columns):
    slots = wave_ref.shape[1]
    slot = slots_of_columns(hi, lax.broadcasted_iota(jnp.int32, (1, columns), 1))
    wave = jnp.broadcast_to(wave_ref[...], (8, slots))
    pick = lax.broadcasted_iota(jnp.int32, (slots, columns), 0) == slot
    pick = jnp.where(pick, 1.0, 0.0).astype(jnp.bfloat16)

    def picked(digits):
        digits = digits.astype(jnp.float32).astype(jnp.bfloat16)
        return jnp.dot(digits, pick, preferred_element_type=jnp.float32)[:1]

    return picked(wave // 16) * 16.0 + picked(wave % 16)


def step_kernel(
    rows, share, steps,
    grid_ref, wave_ref, diagonal_ref, lower_ref, vertical_ref, out_ref,
    grid, basis, u_ref, v_ref, right_in, left_in, right_out, left_out, packed, total,
    parts, wide, spread, sending, gathered,
    table, base_cos, base_sin, near_cos, near_sin,
    diagonal, lower, band, levels_pad, mix, spectra, banded, mixed_early,
    grid_sem, grid_send, right_send, right_recv, left_send, left_recv,
    pack_send, part_sem, plane_send, plane_sem,
):
    x, hi, core, lo, y = place()
    mine = (x * CORE + core) * Y + y
    lat_local, lon_local = grid_ref.shape[1:]
    half = basis.shape[1] // 2
    width = half // DESTS
    f32, bf16 = jnp.float32, jnp.bfloat16

    def peer(offset):
        other = (mine + offset) % PLANE
        return other, device(other // (CORE * Y), hi, other // Y % CORE, lo, other % Y)

    barrier = pltpu.get_barrier_semaphore()

    def greet_line(offset, carry):
        z = (hi * ZLO + lo + offset) % (ZHI * ZLO)
        pl.semaphore_signal(
            barrier, inc=1, device_id=device(x, z // ZLO, core, z % ZLO, y), device_id_type=MESH
        )
        return carry

    def greet_plane(offset, carry):
        pl.semaphore_signal(barrier, inc=1, device_id=peer(offset)[1], device_id_type=MESH)
        return carry

    lax.fori_loop(1, ZHI * ZLO, greet_line, 0)
    lax.fori_loop(1, PLANE, greet_plane, 0)
    pl.semaphore_wait(barrier, ZHI * ZLO - 1 + PLANE - 1)

    def first_row(owner):
        return jnp.minimum(owner * share, rows - share)

    def grid_copies(step):
        columns = pl.ds(pl.multiple_of(y * lon_local, lon_local), lon_local)
        target = grid.at[pl.ds(step * ROWS, ROWS), :, columns]
        for offset in range(1, Y):
            owner = (y + offset) % Y
            pltpu.make_async_remote_copy(
                src_ref=grid_ref.at[pl.ds(first_row(owner) + step * ROWS, ROWS)],
                dst_ref=target,
                send_sem=grid_send,
                recv_sem=grid_sem.at[step],
                device_id=device(x, hi, core, lo, owner),
                device_id_type=MESH,
            ).start()
        pltpu.make_async_copy(
            grid_ref.at[pl.ds(first_row(y) + step * ROWS, ROWS)], target, grid_sem.at[step]
        ).start()

    for step in range(FIRST):
        grid_copies(step)

    waves = waves_of_columns(wave_ref, hi, basis.shape[1])
    column = lax.broadcasted_iota(jnp.int32, (1, basis.shape[1]), 1)
    sine = jnp.where(column // PLANE % 2 == 1, 1.0, 0.0)
    lon, grid_lon = basis.shape[0], basis.shape[0] * ZLO
    coarse, fine = u_ref.shape[0], lon // u_ref.shape[0]
    scale = math.sqrt(2.0 / grid_lon)
    first = (lo * lon + fine * lax.broadcasted_iota(jnp.int32, (coarse, 1), 0)).astype(f32)
    base = waves * first - sine * (grid_lon // 4)
    u_ref[...] = cosine(base, grid_lon) * scale
    v_ref[...] = cosine(base + grid_lon // 4, grid_lon) * scale
    near = waves * lax.broadcasted_iota(jnp.int32, (fine, 1), 0).astype(f32)
    fine_cos, fine_sin = cosine(near, grid_lon), cosine(near - grid_lon // 4, grid_lon)

    def fill(a, carry):
        piece = u_ref[pl.ds(a, 1), :] * fine_cos + v_ref[pl.ds(a, 1), :] * fine_sin
        basis[pl.ds(pl.multiple_of(a * fine, fine), fine), :] = piece.astype(bf16)
        return carry

    lax.fori_loop(0, coarse, fill, 0)
    for step in range(FIRST, AHEAD):
        grid_copies(step)

    def product(step, side):
        left = grid[pl.ds(step * ROWS, ROWS)].reshape(ROWS * lat_local, grid.shape[2])
        return jnp.dot(
            left, basis[:, side * half : (side + 1) * half], preferred_element_type=f32
        )

    def hand_out(step, side):
        for pair in range(DESTS // 2):
            lanes = slice(pair * 2 * width, (pair + 1) * 2 * width)
            top, low = total[side, :lat_local, lanes], total[side, lat_local:, lanes]
            for odd in range(2):
                part = slice(odd * width, (odd + 1) * width)
                packed[step, pair * 2 + odd] = jnp.concatenate(
                    [top[:, part], low[:, part]], axis=1
                ).astype(bf16)
        own_lo = ZLO - 1 if side else 0
        for dest in range(DESTS):
            to_hi = (hi + GROUP_STEP[side][dest]) % ZHI
            to_lo = GROUP_PLACE[side][dest]
            if GROUP_STEP[side][dest] == 0 and to_lo == own_lo:
                pltpu.make_async_copy(
                    packed.at[step, dest], parts.at[step, hi], part_sem.at[step]
                ).start()
            else:
                pltpu.make_async_remote_copy(
                    src_ref=packed.at[step, dest],
                    dst_ref=parts.at[step, hi],
                    send_sem=pack_send,
                    recv_sem=part_sem.at[step],
                    device_id=device(x, to_hi, core, to_lo, y),
                    device_id_type=MESH,
                ).start()

    def chain(step, side):
        arrived, leaving = (right_in, right_out) if side else (left_in, left_out)
        send_sem, recv_sem = (right_send, right_recv) if side else (left_send, left_recv)
        first, last = (0, ZLO - 1) if side else (ZLO - 1, 0)
        row = step % ROWS
        sums = total.at[side, pl.ds(pl.multiple_of(row * lat_local, lat_local), lat_local)]

        @pl.when(row == 0)
        def _():
            total[side] = product(step // ROWS, side)

        @pl.when(lo != first)
        def _():
            pltpu.make_async_copy(arrived.at[step], arrived.at[step], recv_sem.at[step]).wait()
            sums[...] += arrived[step].astype(f32)

        @pl.when(lo != last)
        def _():
            leaving[step] = sums[...].astype(bf16)
            pltpu.make_async_remote_copy(
                src_ref=leaving.at[step],
                dst_ref=arrived.at[step],
                send_sem=send_sem,
                recv_sem=recv_sem.at[step],
                device_id=device(x, hi, core, lo + (1 if side else -1), y),
                device_id_type=MESH,
            ).start()

        @pl.when((lo == last) & (row == ROWS - 1))
        def _():
            hand_out(step // ROWS, side)

    span = ZHI * lat_local
    depth = sending.shape[1]
    tall = 4 * GROUP

    def turn(step):
        pltpu.make_async_copy(parts.at[step], parts.at[step], part_sem.at[step]).wait()
        wide[:span, :] = parts[step].reshape(span, 128).astype(f32)
        turned = wide[...].T
        for group in range(4):
            for part in range(2):
                spread[part, pl.ds(4 * step + group, PLANE, stride=depth), :] = turned[
                    group * PLANE : (group + 1) * PLANE, part * 128 : (part + 1) * 128
                ]

    def through_plane(group):
        at = pl.ds(pl.multiple_of(group * tall, tall), tall)

        def narrow(other):
            begin = pl.multiple_of(other * depth + group * tall, tall)
            for part in range(2):
                sending[other, at, part * 128 : (part + 1) * 128] = spread[
                    part, pl.ds(begin, tall), :
                ].astype(bf16)

        def send(offset, carry):
            other, where = peer(offset)
            narrow(other)
            pltpu.make_async_remote_copy(
                src_ref=sending.at[other, at],
                dst_ref=gathered.at[mine, at],
                send_sem=plane_send,
                recv_sem=plane_sem.at[group],
                device_id=where,
                device_id_type=MESH,
            ).start()
            return carry

        lax.fori_loop(1, PLANE, send, 0)
        narrow(mine)
        pltpu.make_async_copy(
            sending.at[mine, at], gathered.at[mine, at], plane_sem.at[group]
        ).start()

    grid_lat = table.shape[1]
    blocks = diagonal_ref.shape[0]
    fields, levels = vertical_ref.shape[:2]
    owners = X * ZHI * CORE
    pairs = blocks // 2

    def start_meridional():
        scale = math.sqrt(2.0 / grid_lat)
        mode = lax.broadcasted_iota(jnp.int32, (1, grid_lat), 1).astype(f32)
        base = 2 * lat_local * lax.broadcasted_iota(jnp.int32, (owners, 1), 0)
        base = base.astype(f32) * mode
        base_cos[...] = cosine(base, 4 * grid_lat) * scale
        base_sin[...] = cosine(base - grid_lat, 4 * grid_lat) * scale
        near = (2 * lax.broadcasted_iota(jnp.int32, (lat_local, 1), 0) + 1).astype(f32) * mode
        near_cos[...] = cosine(near, 4 * grid_lat)
        near_sin[...] = cosine(near - grid_lat, 4 * grid_lat)
        wide[...] = jnp.zeros_like(wide)
        for row in range(4 * steps, depth):
            for part in range(2):
                spread[part, pl.ds(row, PLANE, stride=depth), :] = jnp.zeros((PLANE, 128), f32)
        for source in range(X * CORE):
            table[source * 256 + span : (source + 1) * 256, :] = jnp.zeros(
                (256 - span, grid_lat), bf16
            )

    def meridional(owner):
        to_x, to_hi, to_core = owner // (ZHI * CORE), owner // CORE % ZHI, owner % CORE
        at = (to_x * CORE + to_core) * 256 + to_hi * lat_local
        piece = base_cos[pl.ds(owner, 1), :] * near_cos[...]
        piece -= base_sin[pl.ds(owner, 1), :] * near_sin[...]
        table[pl.ds(pl.multiple_of(at, 16), lat_local), :] = piece.astype(bf16)

    def squares(lanes):
        tile = pl.ds(pl.multiple_of(lanes * 128, 128), 128)
        for flat, square in ((diagonal_ref, diagonal), (lower_ref, lower)):
            piece = flat[:, tile].astype(f32)
            square[pl.ds(2 * lanes, flat.shape[0], stride=BLK), :] = piece
            square[pl.ds(2 * lanes + 1, flat.shape[0], stride=BLK), :] = pltpu.roll(piece, 64, 1)

    def square(ref, block):
        return ref[pl.ds(pl.multiple_of(block * BLK, BLK), BLK), :][:, :BLK]

    def band_pair(pair):
        one, two = 2 * pair, 2 * pair + 1
        empty = jnp.zeros((BLK, BLK), f32)
        before = jnp.where(pair > 0, square(lower, jnp.maximum(one - 1, 0)), 0.0)
        after = square(lower, jnp.minimum(two, blocks - 2)).T
        after = jnp.where(two < blocks - 1, after, 0.0)
        inner = square(lower, one)
        top = (empty, before, square(diagonal, one), inner.T, empty, empty)
        low = (empty, empty, inner, square(diagonal, two), after, empty)
        band[pair, :BLK, :] = jnp.concatenate(top, axis=1).astype(bf16)
        band[pair, BLK:, :] = jnp.concatenate(low, axis=1).astype(bf16)

    held = mix.shape[1]
    early = depth - tall

    def mixing():
        at = lax.broadcasted_iota(jnp.int32, (1, held), 1)
        rest = at - Y * early
        owner = jnp.where(rest < 0, at // early, rest // tall)
        within = jnp.where(rest < 0, at % early, early + rest % tall)
        row = jnp.minimum(owner * share, rows - share) + within // 2
        fresh = (row >= owner * share) & (within < 2 * share)
        level = lax.broadcasted_iota(jnp.int32, (BLK, 1), 0)
        for field in range(fields):
            levels_pad[...] = jnp.zeros_like(levels_pad)
            levels_pad[:levels, :levels] = vertical_ref[field].astype(f32)
            turned = levels_pad[...].T[:BLK, :].astype(bf16)
            pick = (row == field * levels + level) & (level < levels) & fresh
            pick = jnp.where(pick, 1.0, 0.0).astype(bf16)
            pick = jnp.concatenate([pick, jnp.zeros((128 - BLK, held), bf16)], axis=0)
            mixed = jnp.dot(turned, pick, preferred_element_type=f32)
            for c in range(2):
                part = (c * fields + field) * BLK
                mix[part : part + BLK, :] = jnp.where(at % 2 == c, mixed, 0.0).astype(bf16)

    fill_steps = SKEW * (ZLO - 1)
    count = (steps + LAG) * ROWS + fill_steps
    duties = (
        (start_meridional, 10, 1, 0),
        (mixing, 11, 1, 0),
        (squares, 12, BLK // 2, 2),
        (meridional, 11, owners, 1),
        (band_pair, 12 + BLK // 4, pairs, 1),
    )

    def one(step, carry):
        @pl.when((step % ROWS == 0) & (step // ROWS + AHEAD < steps))
        def _():
            grid_copies(step // ROWS + AHEAD)

        first = step - SKEW * jnp.minimum(lo, ZLO - 1 - lo)

        @pl.when((first >= 0) & (first < steps * ROWS) & (first % ROWS == 0))
        def _():
            block = grid.at[pl.ds(first, ROWS)]
            pltpu.make_async_copy(block, block, grid_sem.at[first // ROWS]).wait()

        for side, here in ((1, lo < ZLO // 2), (0, lo >= 0), (1, lo >= ZLO // 2)):
            at = step - SKEW * (lo if side else ZLO - 1 - lo)

            @pl.when(here & (at >= 0) & (at < steps * ROWS))
            def _():
                chain(at, side)

        ahead = step - fill_steps - (ROWS - 1) - LAG * ROWS
        done = ahead // ROWS

        @pl.when((ahead >= 0) & (ahead % ROWS == 0))
        def _():
            turn(done)

            @pl.when((done % GROUP == GROUP - 1) | (done == steps - 1))
            def _():
                through_plane(done // GROUP)

        for duty, begin, number, each in duties:
            if each:

                @pl.when((step >= begin) & (step < begin + number // each))
                def _():
                    for extra in range(each):
                        duty((step - begin) * each + extra)
            else:

                @pl.when(step == begin)
                def _():
                    duty()

        return carry

    lax.fori_loop(0, count, one, 0)

    sent = grid_ref.at[pl.ds(0, (Y - 1) * share)]
    pltpu.make_async_copy(sent, sent, grid_send).wait()

    @pl.when(lo != ZLO - 1)
    def _():
        pltpu.make_async_copy(right_out, right_out, right_send).wait()

    @pl.when(lo != 0)
    def _():
        pltpu.make_async_copy(left_out, left_out, left_send).wait()

    @pl.when((lo == 0) | (lo == ZLO - 1))
    def _():
        sent = packed.at[:, pl.ds(0, DESTS - 1)]
        pltpu.make_async_copy(sent, sent, pack_send).wait()

    groups = depth // tall
    for begin, end in ((0, groups - 1), (groups - 1, groups)):
        for group in range(begin, end):
            block = gathered.at[:, pl.ds(group * tall, tall)]
            pltpu.make_async_copy(block, block, plane_sem.at[group]).wait()
        high = Y * (end - begin) * tall
        at = slice(Y * begin * tall, Y * end * tall)
        left = jnp.concatenate(
            [
                gathered[source * Y : (source + 1) * Y, begin * tall : end * tall].reshape(high, 256)
                for source in range(X * CORE)
            ],
            axis=1,
        )
        for tile in range(grid_lat // 512):
            lanes = slice(tile * 512, (tile + 1) * 512)
            term = jnp.dot(left, table[:, lanes], preferred_element_type=f32)
            spectra[at, lanes] = term.astype(bf16)
        for pair in range(pairs):
            low, top = max(0, pair - 1) * 128, min(pairs, pair + 2) * 128
            skip = 0 if pair else 128
            banded[at, pair * 128 : (pair + 1) * 128] = lax.dot_general(
                spectra[at, low:top],
                band[pair, :, skip : skip + top - low],
                (((1,), (1,)), ((), ())),
                preferred_element_type=f32,
            ).astype(bf16)
        for tile in range(grid_lat // 512):
            lanes = slice(tile * 512, (tile + 1) * 512)
            result = jnp.dot(mix[:, at], banded[at, lanes], preferred_element_type=f32)
            if begin == 0:
                mixed_early[:, lanes] = result
                continue
            result += mixed_early[:, lanes]
            for c in range(2):
                for field in range(fields):
                    row = (c * fields + field) * BLK
                    out_ref[c, field, :, lanes] = result[row : row + levels].astype(out_ref.dtype)

    sent = sending.at[pl.ds(0, PLANE - 1)]
    pltpu.make_async_copy(sent, sent, plane_send).wait()


def per_device(cotangent, wave_order, band_diagonal, band_lower, vertical_matrix):
    fields, levels, lat_local, lon_local = cotangent.shape
    rows = fields * levels
    grid_lat = lat_local * X * ZHI * CORE
    lon = lon_local * Y
    share = -(-rows // (Y * ROWS)) * ROWS
    steps = share // ROWS
    columns = 2 * wave_order.size
    half = columns // 2
    packed = (lat_local, ROWS * half // DESTS)
    tall = 4 * GROUP
    depth = -(-2 * share // tall) * tall
    owners = X * ZHI * CORE
    blocks = band_diagonal.shape[1]
    f32, bf16 = jnp.float32, jnp.bfloat16
    chain = pltpu.VMEM((steps * ROWS, lat_local, half), bf16)
    hbm = pl.BlockSpec(memory_space=pl.ANY)
    vmem = pl.BlockSpec(memory_space=pltpu.VMEM)
    dma = pltpu.SemaphoreType.DMA
    return pl.pallas_call(
        functools.partial(step_kernel, rows, share, steps),
        out_shape=jax.ShapeDtypeStruct((2, fields, levels, grid_lat), bf16),
        in_specs=[hbm] + [vmem] * 4,
        out_specs=vmem,
        scratch_shapes=[
            pltpu.VMEM((share, lat_local, lon), bf16),
            pltpu.VMEM((lon, columns), bf16),
            pltpu.VMEM((COARSE, columns), f32),
            pltpu.VMEM((COARSE, columns), f32),
            chain,
            chain,
            chain,
            chain,
            pltpu.VMEM((steps, DESTS) + packed, bf16),
            pltpu.VMEM((SIDES, ROWS * lat_local, half), f32),
            pltpu.VMEM((steps, ZHI) + packed, bf16),
            pltpu.VMEM((256, 128), f32),
            pltpu.VMEM((2, PLANE * depth, 128), f32),
            pltpu.VMEM((PLANE, depth, 256), bf16),
            pltpu.VMEM((PLANE, depth, 256), bf16),
            pltpu.VMEM((X * CORE * 256, grid_lat), bf16),
            pltpu.VMEM((owners, grid_lat), f32),
            pltpu.VMEM((owners, grid_lat), f32),
            pltpu.VMEM((lat_local, grid_lat), f32),
            pltpu.VMEM((lat_local, grid_lat), f32),
            pltpu.VMEM((blocks * BLK, 128), f32),
            pltpu.VMEM(((blocks - 1) * BLK, 128), f32),
            pltpu.VMEM((blocks // 2, 2 * BLK, 6 * BLK), bf16),
            pltpu.VMEM((128, 128), f32),
            pltpu.VMEM((2 * fields * BLK, Y * depth), bf16),
            pltpu.VMEM((Y * depth, grid_lat), bf16),
            pltpu.VMEM((Y * depth, grid_lat), bf16),
            pltpu.VMEM((2 * fields * BLK, grid_lat), f32),
            dma((steps,)),
            dma,
            dma,
            dma((steps * ROWS,)),
            dma,
            dma((steps * ROWS,)),
            dma,
            dma((steps,)),
            dma,
            dma((depth // tall,)),
        ],
        compiler_params=pltpu.CompilerParams(
            collective_id=0, has_side_effects=True, vmem_limit_bytes=52 << 20
        ),
    )(
        cotangent.reshape(rows, lat_local, lon_local),
        wave_order.reshape(1, -1),
        band_diagonal[0],
        band_lower[0],
        vertical_matrix,
    )[None]


def solution(mesh):
    return jax.shard_map(
        per_device,
        mesh=mesh,
        in_specs=(
            P(None, None, "lat", "lon"),
            P(),
            P(("lat", "lon"), None, None),
            P(("lat", "lon"), None, None),
            P(),
        ),
        out_specs=P(("lat", "lon"), None, None, None, None),
        check_vma=False,
    )
```

```python
import functools
import math

import jax
import jax.numpy as jnp
from jax import lax
from jax.experimental import pallas as pl
from jax.experimental.pallas import tpu as pltpu
from jax.sharding import PartitionSpec as P

BLK = 64
MESH = pl.DeviceIdType.MESH

X, ZHI, CORE, ZLO, Y = 4, 4, 2, 4, 4
PLANE = X * CORE * Y
GROUP = 4
SIDES, DESTS = 2, 8
GROUP_STEP = ((3, 3, 3, 3, 2, 2, 0, 0), (1, 1, 1, 1, 2, 2, 0, 0))
GROUP_PLACE = ((0, 1, 2, 3, 2, 3, 0, 1), (0, 1, 2, 3, 0, 1, 2, 3))
ROWS = 2
FIRST = 2
AHEAD = 2
LAG = 4
COARSE = 32
SKEW = 3


def place():
    lat, lon = lax.axis_index("lat"), lax.axis_index("lon")
    return lat // (ZHI * CORE), lat // CORE % ZHI, lat % CORE, lon // Y, lon % Y


def device(x, hi, core, lo, y):
    return ((x * ZHI + hi) * CORE + core, lo * Y + y)


def cosine(phase, period):
    quarter = period // 4
    turns = jnp.floor(phase * (1.0 / quarter) + 0.5)
    angle = (phase - turns * quarter) * (2.0 * math.pi / period)
    square = angle * angle
    even = 1.0 + square * (
        -1 / 2 + square * (1 / 24 + square * (-1 / 720 + square * (1 / 40320)))
    )
    odd = angle * (
        1.0 + square * (-1 / 6 + square * (1 / 120 + square * (-1 / 5040 + square * (1 / 362880))))
    )
    turn = turns.astype(jnp.int32) & 3
    value = jnp.where((turn & 1) == 1, odd, even)
    return jnp.where((turn == 1) | (turn == 2), -value, value)


def slots_of_columns(hi, column):
    width = 2 * PLANE
    side, dest, plane = column // (DESTS * width), column // width % DESTS, column % PLANE
    step = jnp.where(dest < 4, jnp.where(side == 0, 3, 1), jnp.where(dest < 6, 2, 0))
    low_side = jnp.where(dest < 4, dest, jnp.where(dest < 6, dest - 2, dest - 6))
    lo = jnp.where(side == 0, low_side, dest % 4)
    lo = jnp.where((side == 1) & (dest >= 6), dest - 4, lo)
    to_hi = (hi + step) % ZHI
    x, core, y = plane // (CORE * Y), plane // Y % CORE, plane % Y
    return (((x * ZHI + to_hi) * CORE + core) * ZLO + lo) * Y + y


def waves_of_columns(wave_ref, hi, columns):
    slots = wave_ref.shape[1]
    slot = slots_of_columns(hi, lax.broadcasted_iota(jnp.int32, (1, columns), 1))
    wave = jnp.broadcast_to(wave_ref[...], (8, slots))
    pick = lax.broadcasted_iota(jnp.int32, (slots, columns), 0) == slot
    pick = jnp.where(pick, 1.0, 0.0).astype(jnp.bfloat16)

    def picked(digits):
        digits = digits.astype(jnp.float32).astype(jnp.bfloat16)
        return jnp.dot(digits, pick, preferred_element_type=jnp.float32)[:1]

    return picked(wave // 16) * 16.0 + picked(wave % 16)


def step_kernel(
    rows, share, steps,
    grid_ref, wave_hbm, diagonal_hbm, lower_hbm, vertical_hbm, out_ref,
    wave_ref, diagonal_ref, lower_ref, vertical_ref,
    grid, basis, u_ref, v_ref, right_in, left_in, right_out, left_out, packed, total,
    parts, wide, spread, sending, gathered,
    table, base_cos, base_sin, near_cos, near_sin,
    diagonal, lower, band, levels_pad, mix, spectra, banded, mixed_early,
    grid_sem, grid_send, right_send, right_recv, left_send, left_recv,
    pack_send, part_sem, plane_send, plane_sem, own_sem,
):
    x, hi, core, lo, y = place()
    mine = (x * CORE + core) * Y + y
    lat_local, lon_local = grid_ref.shape[1:]
    half = basis.shape[1] // 2
    width = half // DESTS
    f32, bf16 = jnp.float32, jnp.bfloat16

    def peer(offset):
        other = (mine + offset) % PLANE
        return other, device(other // (CORE * Y), hi, other // Y % CORE, lo, other % Y)

    own = [
        pltpu.make_async_copy(there, here, own_sem.at[number])
        for number, (there, here) in enumerate(
            (
                (wave_hbm, wave_ref),
                (diagonal_hbm, diagonal_ref),
                (lower_hbm, lower_ref),
                (vertical_hbm, vertical_ref),
            )
        )
    ]
    barrier = pltpu.get_barrier_semaphore()

    def greet_line(offset, carry):
        z = (hi * ZLO + lo + offset) % (ZHI * ZLO)
        pl.semaphore_signal(
            barrier, inc=1, device_id=device(x, z // ZLO, core, z % ZLO, y), device_id_type=MESH
        )
        return carry

    def greet_plane(offset, carry):
        pl.semaphore_signal(barrier, inc=1, device_id=peer(offset)[1], device_id_type=MESH)
        return carry

    lax.fori_loop(1, ZHI * ZLO, greet_line, 0)
    lax.fori_loop(1, PLANE, greet_plane, 0)
    for copy in own:
        copy.start()
    pl.semaphore_wait(barrier, ZHI * ZLO - 1 + PLANE - 1)

    def first_row(owner):
        return jnp.minimum(owner * share, rows - share)

    def grid_copies(step):
        columns = pl.ds(pl.multiple_of(y * lon_local, lon_local), lon_local)
        target = grid.at[pl.ds(step * ROWS, ROWS), :, columns]
        for offset in range(1, Y):
            owner = (y + offset) % Y
            pltpu.make_async_remote_copy(
                src_ref=grid_ref.at[pl.ds(first_row(owner) + step * ROWS, ROWS)],
                dst_ref=target,
                send_sem=grid_send,
                recv_sem=grid_sem.at[step],
                device_id=device(x, hi, core, lo, owner),
                device_id_type=MESH,
            ).start()
        pltpu.make_async_copy(
            grid_ref.at[pl.ds(first_row(y) + step * ROWS, ROWS)], target, grid_sem.at[step]
        ).start()

    for step in range(FIRST):
        grid_copies(step)

    own[0].wait()
    waves = waves_of_columns(wave_ref, hi, basis.shape[1])
    column = lax.broadcasted_iota(jnp.int32, (1, basis.shape[1]), 1)
    sine = jnp.where(column // PLANE % 2 == 1, 1.0, 0.0)
    lon, grid_lon = basis.shape[0], basis.shape[0] * ZLO
    coarse, fine = u_ref.shape[0], lon // u_ref.shape[0]
    scale = math.sqrt(2.0 / grid_lon)
    first = (lo * lon + fine * lax.broadcasted_iota(jnp.int32, (coarse, 1), 0)).astype(f32)
    base = waves * first - sine * (grid_lon // 4)
    u_ref[...] = cosine(base, grid_lon) * scale
    v_ref[...] = cosine(base + grid_lon // 4, grid_lon) * scale
    near = waves * lax.broadcasted_iota(jnp.int32, (fine, 1), 0).astype(f32)
    fine_cos, fine_sin = cosine(near, grid_lon), cosine(near - grid_lon // 4, grid_lon)

    def fill(a, carry):
        piece = u_ref[pl.ds(a, 1), :] * fine_cos + v_ref[pl.ds(a, 1), :] * fine_sin
        basis[pl.ds(pl.multiple_of(a * fine, fine), fine), :] = piece.astype(bf16)
        return carry

    lax.fori_loop(0, coarse, fill, 0)
    for copy in own[1:]:
        copy.wait()
    for step in range(FIRST, AHEAD):
        grid_copies(step)

    def product(step, side):
        left = grid[pl.ds(step * ROWS, ROWS)].reshape(ROWS * lat_local, grid.shape[2])
        return jnp.dot(
            left, basis[:, side * half : (side + 1) * half], preferred_element_type=f32
        )

    def hand_out(step, side):
        for pair in range(DESTS // 2):
            lanes = slice(pair * 2 * width, (pair + 1) * 2 * width)
            top, low = total[side, :lat_local, lanes], total[side, lat_local:, lanes]
            for odd in range(2):
                part = slice(odd * width, (odd + 1) * width)
                packed[step, pair * 2 + odd] = jnp.concatenate(
                    [top[:, part], low[:, part]], axis=1
                ).astype(bf16)
        own_lo = ZLO - 1 if side else 0
        for dest in range(DESTS):
            to_hi = (hi + GROUP_STEP[side][dest]) % ZHI
            to_lo = GROUP_PLACE[side][dest]
            if GROUP_STEP[side][dest] == 0 and to_lo == own_lo:
                pltpu.make_async_copy(
                    packed.at[step, dest], parts.at[step, hi], part_sem.at[step]
                ).start()
            else:
                pltpu.make_async_remote_copy(
                    src_ref=packed.at[step, dest],
                    dst_ref=parts.at[step, hi],
                    send_sem=pack_send,
                    recv_sem=part_sem.at[step],
                    device_id=device(x, to_hi, core, to_lo, y),
                    device_id_type=MESH,
                ).start()

    def chain(step, side):
        arrived, leaving = (right_in, right_out) if side else (left_in, left_out)
        send_sem, recv_sem = (right_send, right_recv) if side else (left_send, left_recv)
        first, last = (0, ZLO - 1) if side else (ZLO - 1, 0)
        row = step % ROWS
        sums = total.at[side, pl.ds(pl.multiple_of(row * lat_local, lat_local), lat_local)]

        @pl.when(row == 0)
        def _():
            total[side] = product(step // ROWS, side)

        @pl.when(lo != first)
        def _():
            pltpu.make_async_copy(arrived.at[step], arrived.at[step], recv_sem.at[step]).wait()
            sums[...] += arrived[step].astype(f32)

        @pl.when(lo != last)
        def _():
            leaving[step] = sums[...].astype(bf16)
            pltpu.make_async_remote_copy(
                src_ref=leaving.at[step],
                dst_ref=arrived.at[step],
                send_sem=send_sem,
                recv_sem=recv_sem.at[step],
                device_id=device(x, hi, core, lo + (1 if side else -1), y),
                device_id_type=MESH,
            ).start()

        @pl.when((lo == last) & (row == ROWS - 1))
        def _():
            hand_out(step // ROWS, side)

    span = ZHI * lat_local
    depth = sending.shape[1]
    tall = 4 * GROUP

    def turn(step):
        pltpu.make_async_copy(parts.at[step], parts.at[step], part_sem.at[step]).wait()
        wide[:span, :] = parts[step].reshape(span, 128).astype(f32)
        turned = wide[...].T
        for group in range(4):
            for part in range(2):
                spread[part, pl.ds(4 * step + group, PLANE, stride=depth), :] = turned[
                    group * PLANE : (group + 1) * PLANE, part * 128 : (part + 1) * 128
                ]

    def through_plane(group):
        at = pl.ds(pl.multiple_of(group * tall, tall), tall)

        def narrow(other):
            begin = pl.multiple_of(other * depth + group * tall, tall)
            for part in range(2):
                sending[other, at, part * 128 : (part + 1) * 128] = spread[
                    part, pl.ds(begin, tall), :
                ].astype(bf16)

        def send(offset, carry):
            other, where = peer(offset)
            narrow(other)
            pltpu.make_async_remote_copy(
                src_ref=sending.at[other, at],
                dst_ref=gathered.at[mine, at],
                send_sem=plane_send,
                recv_sem=plane_sem.at[group],
                device_id=where,
                device_id_type=MESH,
            ).start()
            return carry

        lax.fori_loop(1, PLANE, send, 0)
        narrow(mine)
        pltpu.make_async_copy(
            sending.at[mine, at], gathered.at[mine, at], plane_sem.at[group]
        ).start()

    grid_lat = table.shape[1]
    blocks = diagonal_ref.shape[0]
    fields, levels = vertical_ref.shape[:2]
    owners = X * ZHI * CORE
    pairs = blocks // 2

    def start_meridional():
        scale = math.sqrt(2.0 / grid_lat)
        mode = lax.broadcasted_iota(jnp.int32, (1, grid_lat), 1).astype(f32)
        base = 2 * lat_local * lax.broadcasted_iota(jnp.int32, (owners, 1), 0)
        base = base.astype(f32) * mode
        base_cos[...] = cosine(base, 4 * grid_lat) * scale
        base_sin[...] = cosine(base - grid_lat, 4 * grid_lat) * scale
        near = (2 * lax.broadcasted_iota(jnp.int32, (lat_local, 1), 0) + 1).astype(f32) * mode
        near_cos[...] = cosine(near, 4 * grid_lat)
        near_sin[...] = cosine(near - grid_lat, 4 * grid_lat)
        wide[...] = jnp.zeros_like(wide)
        for row in range(4 * steps, depth):
            for part in range(2):
                spread[part, pl.ds(row, PLANE, stride=depth), :] = jnp.zeros((PLANE, 128), f32)
        for source in range(X * CORE):
            table[source * 256 + span : (source + 1) * 256, :] = jnp.zeros(
                (256 - span, grid_lat), bf16
            )

    def meridional(owner):
        to_x, to_hi, to_core = owner // (ZHI * CORE), owner // CORE % ZHI, owner % CORE
        at = (to_x * CORE + to_core) * 256 + to_hi * lat_local
        piece = base_cos[pl.ds(owner, 1), :] * near_cos[...]
        piece -= base_sin[pl.ds(owner, 1), :] * near_sin[...]
        table[pl.ds(pl.multiple_of(at, 16), lat_local), :] = piece.astype(bf16)

    def squares(lanes):
        tile = pl.ds(pl.multiple_of(lanes * 128, 128), 128)
        for flat, square in ((diagonal_ref, diagonal), (lower_ref, lower)):
            piece = flat[:, tile].astype(f32)
            square[pl.ds(2 * lanes, flat.shape[0], stride=BLK), :] = piece
            square[pl.ds(2 * lanes + 1, flat.shape[0], stride=BLK), :] = pltpu.roll(piece, 64, 1)

    def square(ref, block):
        return ref[pl.ds(pl.multiple_of(block * BLK, BLK), BLK), :][:, :BLK]

    def band_pair(pair):
        one, two = 2 * pair, 2 * pair + 1
        empty = jnp.zeros((BLK, BLK), f32)
        before = jnp.where(pair > 0, square(lower, jnp.maximum(one - 1, 0)), 0.0)
        after = square(lower, jnp.minimum(two, blocks - 2)).T
        after = jnp.where(two < blocks - 1, after, 0.0)
        inner = square(lower, one)
        top = (empty, before, square(diagonal, one), inner.T, empty, empty)
        low = (empty, empty, inner, square(diagonal, two), after, empty)
        band[pair, :BLK, :] = jnp.concatenate(top, axis=1).astype(bf16)
        band[pair, BLK:, :] = jnp.concatenate(low, axis=1).astype(bf16)

    held = mix.shape[1]
    early = depth - tall

    def mixing():
        at = lax.broadcasted_iota(jnp.int32, (1, held), 1)
        rest = at - Y * early
        owner = jnp.where(rest < 0, at // early, rest // tall)
        within = jnp.where(rest < 0, at % early, early + rest % tall)
        row = jnp.minimum(owner * share, rows - share) + within // 2
        fresh = (row >= owner * share) & (within < 2 * share)
        level = lax.broadcasted_iota(jnp.int32, (BLK, 1), 0)
        for field in range(fields):
            levels_pad[...] = jnp.zeros_like(levels_pad)
            levels_pad[:levels, :levels] = vertical_ref[field].astype(f32)
            turned = levels_pad[...].T[:BLK, :].astype(bf16)
            pick = (row == field * levels + level) & (level < levels) & fresh
            pick = jnp.where(pick, 1.0, 0.0).astype(bf16)
            pick = jnp.concatenate([pick, jnp.zeros((128 - BLK, held), bf16)], axis=0)
            mixed = jnp.dot(turned, pick, preferred_element_type=f32)
            for c in range(2):
                part = (c * fields + field) * BLK
                mix[part : part + BLK, :] = jnp.where(at % 2 == c, mixed, 0.0).astype(bf16)

    fill_steps = SKEW * (ZLO - 1)
    count = (steps + LAG) * ROWS + fill_steps
    duties = (
        (start_meridional, 10, 1, 0),
        (mixing, 11, 1, 0),
        (squares, 12, BLK // 2, 2),
        (meridional, 11, owners, 1),
        (band_pair, 12 + BLK // 4, pairs, 1),
    )

    def one(step, carry):
        @pl.when((step % ROWS == 0) & (step // ROWS + AHEAD < steps))
        def _():
            grid_copies(step // ROWS + AHEAD)

        first = step - SKEW * jnp.minimum(lo, ZLO - 1 - lo)

        @pl.when((first >= 0) & (first < steps * ROWS) & (first % ROWS == 0))
        def _():
            block = grid.at[pl.ds(first, ROWS)]
            pltpu.make_async_copy(block, block, grid_sem.at[first // ROWS]).wait()

        for side, here in ((1, lo < ZLO // 2), (0, lo >= 0), (1, lo >= ZLO // 2)):
            at = step - SKEW * (lo if side else ZLO - 1 - lo)

            @pl.when(here & (at >= 0) & (at < steps * ROWS))
            def _():
                chain(at, side)

        ahead = step - fill_steps - (ROWS - 1) - LAG * ROWS
        done = ahead // ROWS

        @pl.when((ahead >= 0) & (ahead % ROWS == 0))
        def _():
            turn(done)

            @pl.when((done % GROUP == GROUP - 1) | (done == steps - 1))
            def _():
                through_plane(done // GROUP)

        for duty, begin, number, each in duties:
            if each:

                @pl.when((step >= begin) & (step < begin + number // each))
                def _():
                    for extra in range(each):
                        duty((step - begin) * each + extra)
            else:

                @pl.when(step == begin)
                def _():
                    duty()

        return carry

    lax.fori_loop(0, count, one, 0)

    sent = grid_ref.at[pl.ds(0, (Y - 1) * share)]
    pltpu.make_async_copy(sent, sent, grid_send).wait()

    @pl.when(lo != ZLO - 1)
    def _():
        pltpu.make_async_copy(right_out, right_out, right_send).wait()

    @pl.when(lo != 0)
    def _():
        pltpu.make_async_copy(left_out, left_out, left_send).wait()

    @pl.when((lo == 0) | (lo == ZLO - 1))
    def _():
        sent = packed.at[:, pl.ds(0, DESTS - 1)]
        pltpu.make_async_copy(sent, sent, pack_send).wait()

    groups = depth // tall
    for begin, end in ((0, groups - 1), (groups - 1, groups)):
        for group in range(begin, end):
            block = gathered.at[:, pl.ds(group * tall, tall)]
            pltpu.make_async_copy(block, block, plane_sem.at[group]).wait()
        high = Y * (end - begin) * tall
        at = slice(Y * begin * tall, Y * end * tall)
        left = jnp.concatenate(
            [
                gathered[source * Y : (source + 1) * Y, begin * tall : end * tall].reshape(high, 256)
                for source in range(X * CORE)
            ],
            axis=1,
        )
        for tile in range(grid_lat // 512):
            lanes = slice(tile * 512, (tile + 1) * 512)
            term = jnp.dot(left, table[:, lanes], preferred_element_type=f32)
            spectra[at, lanes] = term.astype(bf16)
        for pair in range(pairs):
            low, top = max(0, pair - 1) * 128, min(pairs, pair + 2) * 128
            skip = 0 if pair else 128
            banded[at, pair * 128 : (pair + 1) * 128] = lax.dot_general(
                spectra[at, low:top],
                band[pair, :, skip : skip + top - low],
                (((1,), (1,)), ((), ())),
                preferred_element_type=f32,
            ).astype(bf16)
        for tile in range(grid_lat // 512):
            lanes = slice(tile * 512, (tile + 1) * 512)
            result = jnp.dot(mix[:, at], banded[at, lanes], preferred_element_type=f32)
            if begin == 0:
                mixed_early[:, lanes] = result
                continue
            result += mixed_early[:, lanes]
            for c in range(2):
                for field in range(fields):
                    row = (c * fields + field) * BLK
                    out_ref[c, field, :, lanes] = result[row : row + levels].astype(out_ref.dtype)

    sent = sending.at[pl.ds(0, PLANE - 1)]
    pltpu.make_async_copy(sent, sent, plane_send).wait()


def per_device(cotangent, wave_order, band_diagonal, band_lower, vertical_matrix):
    fields, levels, lat_local, lon_local = cotangent.shape
    rows = fields * levels
    grid_lat = lat_local * X * ZHI * CORE
    lon = lon_local * Y
    share = -(-rows // (Y * ROWS)) * ROWS
    steps = share // ROWS
    columns = 2 * wave_order.size
    half = columns // 2
    packed = (lat_local, ROWS * half // DESTS)
    tall = 4 * GROUP
    depth = -(-2 * share // tall) * tall
    owners = X * ZHI * CORE
    blocks = band_diagonal.shape[1]
    f32, bf16 = jnp.float32, jnp.bfloat16
    chain = pltpu.VMEM((steps * ROWS, lat_local, half), bf16)
    hbm = pl.BlockSpec(memory_space=pl.ANY)
    vmem = pl.BlockSpec(memory_space=pltpu.VMEM)
    dma = pltpu.SemaphoreType.DMA
    return pl.pallas_call(
        functools.partial(step_kernel, rows, share, steps),
        out_shape=pltpu.VMEM((2, fields, levels, grid_lat), bf16),
        in_specs=[hbm] * 5,
        out_specs=vmem,
        scratch_shapes=[
            pltpu.VMEM((1, wave_order.size), jnp.int32),
            pltpu.VMEM(band_diagonal.shape[1:], bf16),
            pltpu.VMEM(band_lower.shape[1:], bf16),
            pltpu.VMEM(vertical_matrix.shape, bf16),
            pltpu.VMEM((share, lat_local, lon), bf16),
            pltpu.VMEM((lon, columns), bf16),
            pltpu.VMEM((COARSE, columns), f32),
            pltpu.VMEM((COARSE, columns), f32),
            chain,
            chain,
            chain,
            chain,
            pltpu.VMEM((steps, DESTS) + packed, bf16),
            pltpu.VMEM((SIDES, ROWS * lat_local, half), f32),
            pltpu.VMEM((steps, ZHI) + packed, bf16),
            pltpu.VMEM((256, 128), f32),
            pltpu.VMEM((2, PLANE * depth, 128), f32),
            pltpu.VMEM((PLANE, depth, 256), bf16),
            pltpu.VMEM((PLANE, depth, 256), bf16),
            pltpu.VMEM((X * CORE * 256, grid_lat), bf16),
            pltpu.VMEM((owners, grid_lat), f32),
            pltpu.VMEM((owners, grid_lat), f32),
            pltpu.VMEM((lat_local, grid_lat), f32),
            pltpu.VMEM((lat_local, grid_lat), f32),
            pltpu.VMEM((blocks * BLK, 128), f32),
            pltpu.VMEM(((blocks - 1) * BLK, 128), f32),
            pltpu.VMEM((blocks // 2, 2 * BLK, 6 * BLK), bf16),
            pltpu.VMEM((128, 128), f32),
            pltpu.VMEM((2 * fields * BLK, Y * depth), bf16),
            pltpu.VMEM((Y * depth, grid_lat), bf16),
            pltpu.VMEM((Y * depth, grid_lat), bf16),
            pltpu.VMEM((2 * fields * BLK, grid_lat), f32),
            dma((steps,)),
            dma,
            dma,
            dma((steps * ROWS,)),
            dma,
            dma((steps * ROWS,)),
            dma,
            dma((steps,)),
            dma,
            dma((depth // tall,)),
            dma((4,)),
        ],
        compiler_params=pltpu.CompilerParams(
            collective_id=0, has_side_effects=True, vmem_limit_bytes=54 << 20
        ),
    )(
        cotangent.reshape(rows, lat_local, lon_local),
        wave_order.reshape(1, -1),
        band_diagonal[0],
        band_lower[0],
        vertical_matrix,
    )[None]


def solution(mesh):
    return jax.shard_map(
        per_device,
        mesh=mesh,
        in_specs=(
            P(None, None, "lat", "lon"),
            P(),
            P(("lat", "lon"), None, None),
            P(("lat", "lon"), None, None),
            P(),
        ),
        out_specs=P(("lat", "lon"), None, None, None, None),
        check_vma=False,
    )
```

```python
import functools
import math

import jax
import jax.numpy as jnp
from jax import lax
from jax.experimental import pallas as pl
from jax.experimental.pallas import tpu as pltpu
from jax.sharding import PartitionSpec as P

BLK = 64
MESH = pl.DeviceIdType.MESH

X, ZHI, CORE, ZLO, Y = 4, 4, 2, 4, 4
PLANE = X * CORE * Y
GROUP = 4
SIDES, DESTS = 2, 8
GROUP_STEP = ((3, 3, 3, 3, 2, 2, 0, 0), (1, 1, 1, 1, 2, 2, 0, 0))
GROUP_PLACE = ((0, 1, 2, 3, 2, 3, 0, 1), (0, 1, 2, 3, 0, 1, 2, 3))
ROWS = 2
FIRST = 2
AHEAD = 2
LAG = 4
COARSE = 32
SKEW = 3


def place():
    lat, lon = lax.axis_index("lat"), lax.axis_index("lon")
    return lat // (ZHI * CORE), lat // CORE % ZHI, lat % CORE, lon // Y, lon % Y


def device(x, hi, core, lo, y):
    return ((x * ZHI + hi) * CORE + core, lo * Y + y)


def cosine(phase, period):
    quarter = period // 4
    turns = jnp.floor(phase * (1.0 / quarter) + 0.5)
    angle = (phase - turns * quarter) * (2.0 * math.pi / period)
    square = angle * angle
    even = 1.0 + square * (
        -1 / 2 + square * (1 / 24 + square * (-1 / 720 + square * (1 / 40320)))
    )
    odd = angle * (
        1.0 + square * (-1 / 6 + square * (1 / 120 + square * (-1 / 5040 + square * (1 / 362880))))
    )
    turn = turns.astype(jnp.int32) & 3
    value = jnp.where((turn & 1) == 1, odd, even)
    return jnp.where((turn == 1) | (turn == 2), -value, value)


def slots_of_columns(hi, column):
    width = 2 * PLANE
    side, dest, plane = column // (DESTS * width), column // width % DESTS, column % PLANE
    step = jnp.where(dest < 4, jnp.where(side == 0, 3, 1), jnp.where(dest < 6, 2, 0))
    low_side = jnp.where(dest < 4, dest, jnp.where(dest < 6, dest - 2, dest - 6))
    lo = jnp.where(side == 0, low_side, dest % 4)
    lo = jnp.where((side == 1) & (dest >= 6), dest - 4, lo)
    to_hi = (hi + step) % ZHI
    x, core, y = plane // (CORE * Y), plane // Y % CORE, plane % Y
    return (((x * ZHI + to_hi) * CORE + core) * ZLO + lo) * Y + y


def waves_of_columns(wave_ref, hi, columns):
    slots = wave_ref.shape[1]
    slot = slots_of_columns(hi, lax.broadcasted_iota(jnp.int32, (1, columns), 1))
    wave = jnp.broadcast_to(wave_ref[...], (8, slots))
    pick = lax.broadcasted_iota(jnp.int32, (slots, columns), 0) == slot
    pick = jnp.where(pick, 1.0, 0.0).astype(jnp.bfloat16)

    def picked(digits):
        digits = digits.astype(jnp.float32).astype(jnp.bfloat16)
        return jnp.dot(digits, pick, preferred_element_type=jnp.float32)[:1]

    return picked(wave // 16) * 16.0 + picked(wave % 16)


def step_kernel(
    rows, share, steps,
    grid_ref, wave_hbm, diagonal_hbm, lower_hbm, vertical_hbm, out_ref,
    wave_ref, diagonal_ref, lower_ref, vertical_ref,
    grid, basis, u_ref, v_ref, right_in, left_in, right_out, left_out, packed, total,
    parts, wide, spread, sending, gathered,
    table, base_cos, base_sin, near_cos, near_sin,
    diagonal, lower, band, levels_pad, mix, spectra, banded, mixed_early, late,
    grid_sem, grid_send, right_send, right_recv, left_send, left_recv,
    pack_send, part_sem, plane_send, plane_sem, own_sem,
):
    x, hi, core, lo, y = place()
    mine = (x * CORE + core) * Y + y
    lat_local, lon_local = grid_ref.shape[1:]
    half = basis.shape[1] // 2
    width = half // DESTS
    f32, bf16 = jnp.float32, jnp.bfloat16

    def peer(offset):
        other = (mine + offset) % PLANE
        return other, device(other // (CORE * Y), hi, other // Y % CORE, lo, other % Y)

    own = [
        pltpu.make_async_copy(there, here, own_sem.at[number])
        for number, (there, here) in enumerate(
            (
                (wave_hbm, wave_ref),
                (diagonal_hbm, diagonal_ref),
                (lower_hbm, lower_ref),
                (vertical_hbm, vertical_ref),
            )
        )
    ]
    barrier = pltpu.get_barrier_semaphore()

    def greet_line(offset, carry):
        z = (hi * ZLO + lo + offset) % (ZHI * ZLO)
        pl.semaphore_signal(
            barrier, inc=1, device_id=device(x, z // ZLO, core, z % ZLO, y), device_id_type=MESH
        )
        return carry

    def greet_plane(offset, carry):
        pl.semaphore_signal(barrier, inc=1, device_id=peer(offset)[1], device_id_type=MESH)
        return carry

    lax.fori_loop(1, ZHI * ZLO, greet_line, 0)
    lax.fori_loop(1, PLANE, greet_plane, 0)
    for copy in own:
        copy.start()
    pl.semaphore_wait(barrier, ZHI * ZLO - 1 + PLANE - 1)

    def first_row(owner):
        return jnp.minimum(owner * share, rows - share)

    def grid_copies(step):
        columns = pl.ds(pl.multiple_of(y * lon_local, lon_local), lon_local)
        target = grid.at[pl.ds(step * ROWS, ROWS), :, columns]
        for offset in range(1, Y):
            owner = (y + offset) % Y
            pltpu.make_async_remote_copy(
                src_ref=grid_ref.at[pl.ds(first_row(owner) + step * ROWS, ROWS)],
                dst_ref=target,
                send_sem=grid_send,
                recv_sem=grid_sem.at[step],
                device_id=device(x, hi, core, lo, owner),
                device_id_type=MESH,
            ).start()
        pltpu.make_async_copy(
            grid_ref.at[pl.ds(first_row(y) + step * ROWS, ROWS)], target, grid_sem.at[step]
        ).start()

    for step in range(FIRST):
        grid_copies(step)

    own[0].wait()
    waves = waves_of_columns(wave_ref, hi, basis.shape[1])
    column = lax.broadcasted_iota(jnp.int32, (1, basis.shape[1]), 1)
    sine = jnp.where(column // PLANE % 2 == 1, 1.0, 0.0)
    lon, grid_lon = basis.shape[0], basis.shape[0] * ZLO
    coarse, fine = u_ref.shape[0], lon // u_ref.shape[0]
    scale = math.sqrt(2.0 / grid_lon)
    first = (lo * lon + fine * lax.broadcasted_iota(jnp.int32, (coarse, 1), 0)).astype(f32)
    base = waves * first - sine * (grid_lon // 4)
    u_ref[...] = cosine(base, grid_lon) * scale
    v_ref[...] = cosine(base + grid_lon // 4, grid_lon) * scale
    near = waves * lax.broadcasted_iota(jnp.int32, (fine, 1), 0).astype(f32)
    fine_cos, fine_sin = cosine(near, grid_lon), cosine(near - grid_lon // 4, grid_lon)

    def fill(a, carry):
        piece = u_ref[pl.ds(a, 1), :] * fine_cos + v_ref[pl.ds(a, 1), :] * fine_sin
        basis[pl.ds(pl.multiple_of(a * fine, fine), fine), :] = piece.astype(bf16)
        return carry

    lax.fori_loop(0, coarse, fill, 0)
    for copy in own[1:]:
        copy.wait()
    for step in range(FIRST, AHEAD):
        grid_copies(step)

    def product(step, side):
        left = grid[pl.ds(step * ROWS, ROWS)].reshape(ROWS * lat_local, grid.shape[2])
        return jnp.dot(
            left, basis[:, side * half : (side + 1) * half], preferred_element_type=f32
        )

    def hand_out(step, side):
        for pair in range(DESTS // 2):
            lanes = slice(pair * 2 * width, (pair + 1) * 2 * width)
            top, low = total[side, :lat_local, lanes], total[side, lat_local:, lanes]
            for odd in range(2):
                part = slice(odd * width, (odd + 1) * width)
                packed[step, pair * 2 + odd] = jnp.concatenate(
                    [top[:, part], low[:, part]], axis=1
                ).astype(bf16)
        own_lo = ZLO - 1 if side else 0
        for dest in range(DESTS):
            to_hi = (hi + GROUP_STEP[side][dest]) % ZHI
            to_lo = GROUP_PLACE[side][dest]
            if GROUP_STEP[side][dest] == 0 and to_lo == own_lo:
                pltpu.make_async_copy(
                    packed.at[step, dest], parts.at[step, hi], part_sem.at[step]
                ).start()
            else:
                pltpu.make_async_remote_copy(
                    src_ref=packed.at[step, dest],
                    dst_ref=parts.at[step, hi],
                    send_sem=pack_send,
                    recv_sem=part_sem.at[step],
                    device_id=device(x, to_hi, core, to_lo, y),
                    device_id_type=MESH,
                ).start()

    def chain(step, side):
        arrived, leaving = (right_in, right_out) if side else (left_in, left_out)
        send_sem, recv_sem = (right_send, right_recv) if side else (left_send, left_recv)
        first, last = (0, ZLO - 1) if side else (ZLO - 1, 0)
        row = step % ROWS
        sums = total.at[side, pl.ds(pl.multiple_of(row * lat_local, lat_local), lat_local)]

        @pl.when(row == 0)
        def _():
            total[side] = product(step // ROWS, side)

        @pl.when(lo != first)
        def _():
            pltpu.make_async_copy(arrived.at[step], arrived.at[step], recv_sem.at[step]).wait()
            sums[...] += arrived[step].astype(f32)

        @pl.when(lo != last)
        def _():
            leaving[step] = sums[...].astype(bf16)
            pltpu.make_async_remote_copy(
                src_ref=leaving.at[step],
                dst_ref=arrived.at[step],
                send_sem=send_sem,
                recv_sem=recv_sem.at[step],
                device_id=device(x, hi, core, lo + (1 if side else -1), y),
                device_id_type=MESH,
            ).start()

        @pl.when((lo == last) & (row == ROWS - 1))
        def _():
            hand_out(step // ROWS, side)

    span = ZHI * lat_local
    depth = sending.shape[1]
    tall = 4 * GROUP

    def turn(step):
        pltpu.make_async_copy(parts.at[step], parts.at[step], part_sem.at[step]).wait()
        wide[:span, :] = parts[step].reshape(span, 128).astype(f32)
        turned = wide[...].T
        for group in range(4):
            for part in range(2):
                spread[part, pl.ds(4 * step + group, PLANE, stride=depth), :] = turned[
                    group * PLANE : (group + 1) * PLANE, part * 128 : (part + 1) * 128
                ]

    groups = depth // tall

    def arrival(group, offset):
        other = (mine + offset) % PLANE
        across = (other // (CORE * Y) + X - x) % X * CORE + (other // Y % CORE + CORE - core) % CORE
        return plane_sem.at[group + group // (groups - 1) * across]

    def through_plane(group):
        at = pl.ds(pl.multiple_of(group * tall, tall), tall)

        def narrow(other):
            begin = pl.multiple_of(other * depth + group * tall, tall)
            for part in range(2):
                sending[other, at, part * 128 : (part + 1) * 128] = spread[
                    part, pl.ds(begin, tall), :
                ].astype(bf16)

        def send(offset, carry):
            other, where = peer(offset)
            narrow(other)
            pltpu.make_async_remote_copy(
                src_ref=sending.at[other, at],
                dst_ref=gathered.at[mine, at],
                send_sem=plane_send,
                recv_sem=arrival(group, offset),
                device_id=where,
                device_id_type=MESH,
            ).start()
            return carry

        lax.fori_loop(1, PLANE, send, 0)
        narrow(mine)
        pltpu.make_async_copy(
            sending.at[mine, at], gathered.at[mine, at], arrival(group, 0)
        ).start()

    grid_lat = table.shape[1]
    blocks = diagonal_ref.shape[0]
    fields, levels = vertical_ref.shape[:2]
    owners = X * ZHI * CORE
    pairs = blocks // 2

    def start_meridional():
        scale = math.sqrt(2.0 / grid_lat)
        mode = lax.broadcasted_iota(jnp.int32, (1, grid_lat), 1).astype(f32)
        base = 2 * lat_local * lax.broadcasted_iota(jnp.int32, (owners, 1), 0)
        base = base.astype(f32) * mode
        base_cos[...] = cosine(base, 4 * grid_lat) * scale
        base_sin[...] = cosine(base - grid_lat, 4 * grid_lat) * scale
        near = (2 * lax.broadcasted_iota(jnp.int32, (lat_local, 1), 0) + 1).astype(f32) * mode
        near_cos[...] = cosine(near, 4 * grid_lat)
        near_sin[...] = cosine(near - grid_lat, 4 * grid_lat)
        wide[...] = jnp.zeros_like(wide)
        for row in range(4 * steps, depth):
            for part in range(2):
                spread[part, pl.ds(row, PLANE, stride=depth), :] = jnp.zeros((PLANE, 128), f32)
        for source in range(X * CORE):
            table[source * 256 + span : (source + 1) * 256, :] = jnp.zeros(
                (256 - span, grid_lat), bf16
            )

    def meridional(owner):
        to_x, to_hi, to_core = owner // (ZHI * CORE), owner // CORE % ZHI, owner % CORE
        at = (to_x * CORE + to_core) * 256 + to_hi * lat_local
        piece = base_cos[pl.ds(owner, 1), :] * near_cos[...]
        piece -= base_sin[pl.ds(owner, 1), :] * near_sin[...]
        table[pl.ds(pl.multiple_of(at, 16), lat_local), :] = piece.astype(bf16)

    def squares(lanes):
        tile = pl.ds(pl.multiple_of(lanes * 128, 128), 128)
        for flat, square in ((diagonal_ref, diagonal), (lower_ref, lower)):
            piece = flat[:, tile].astype(f32)
            square[pl.ds(2 * lanes, flat.shape[0], stride=BLK), :] = piece
            square[pl.ds(2 * lanes + 1, flat.shape[0], stride=BLK), :] = pltpu.roll(piece, 64, 1)

    def square(ref, block):
        return ref[pl.ds(pl.multiple_of(block * BLK, BLK), BLK), :][:, :BLK]

    def band_pair(pair):
        one, two = 2 * pair, 2 * pair + 1
        empty = jnp.zeros((BLK, BLK), f32)
        before = jnp.where(pair > 0, square(lower, jnp.maximum(one - 1, 0)), 0.0)
        after = square(lower, jnp.minimum(two, blocks - 2)).T
        after = jnp.where(two < blocks - 1, after, 0.0)
        inner = square(lower, one)
        top = (empty, before, square(diagonal, one), inner.T, empty, empty)
        low = (empty, empty, inner, square(diagonal, two), after, empty)
        band[pair, :BLK, :] = jnp.concatenate(top, axis=1).astype(bf16)
        band[pair, BLK:, :] = jnp.concatenate(low, axis=1).astype(bf16)

    held = mix.shape[1]
    early = depth - tall

    def mixing():
        at = lax.broadcasted_iota(jnp.int32, (1, held), 1)
        rest = at - Y * early
        owner = jnp.where(rest < 0, at // early, rest // tall)
        within = jnp.where(rest < 0, at % early, early + rest % tall)
        row = jnp.minimum(owner * share, rows - share) + within // 2
        fresh = (row >= owner * share) & (within < 2 * share)
        level = lax.broadcasted_iota(jnp.int32, (BLK, 1), 0)
        for field in range(fields):
            levels_pad[...] = jnp.zeros_like(levels_pad)
            levels_pad[:levels, :levels] = vertical_ref[field].astype(f32)
            turned = levels_pad[...].T[:BLK, :].astype(bf16)
            pick = (row == field * levels + level) & (level < levels) & fresh
            pick = jnp.where(pick, 1.0, 0.0).astype(bf16)
            pick = jnp.concatenate([pick, jnp.zeros((128 - BLK, held), bf16)], axis=0)
            mixed = jnp.dot(turned, pick, preferred_element_type=f32)
            for c in range(2):
                part = (c * fields + field) * BLK
                mix[part : part + BLK, :] = jnp.where(at % 2 == c, mixed, 0.0).astype(bf16)

    fill_steps = SKEW * (ZLO - 1)
    count = (steps + LAG) * ROWS + fill_steps
    duties = (
        (start_meridional, 10, 1, 0),
        (mixing, 11, 1, 0),
        (squares, 12, BLK // 2, 2),
        (meridional, 11, owners, 1),
        (band_pair, 12 + BLK // 4, pairs, 1),
    )

    def one(step, carry):
        @pl.when((step % ROWS == 0) & (step // ROWS + AHEAD < steps))
        def _():
            grid_copies(step // ROWS + AHEAD)

        first = step - SKEW * jnp.minimum(lo, ZLO - 1 - lo)

        @pl.when((first >= 0) & (first < steps * ROWS) & (first % ROWS == 0))
        def _():
            block = grid.at[pl.ds(first, ROWS)]
            pltpu.make_async_copy(block, block, grid_sem.at[first // ROWS]).wait()

        for side, here in ((1, lo < ZLO // 2), (0, lo >= 0), (1, lo >= ZLO // 2)):
            at = step - SKEW * (lo if side else ZLO - 1 - lo)

            @pl.when(here & (at >= 0) & (at < steps * ROWS))
            def _():
                chain(at, side)

        ahead = step - fill_steps - (ROWS - 1) - LAG * ROWS
        done = ahead // ROWS

        @pl.when((ahead >= 0) & (ahead % ROWS == 0))
        def _():
            turn(done)

            @pl.when((done % GROUP == GROUP - 1) | (done == steps - 1))
            def _():
                through_plane(done // GROUP)

        for duty, begin, number, each in duties:
            if each:

                @pl.when((step >= begin) & (step < begin + number // each))
                def _():
                    for extra in range(each):
                        duty((step - begin) * each + extra)
            else:

                @pl.when(step == begin)
                def _():
                    duty()

        return carry

    lax.fori_loop(0, count, one, 0)

    sent = grid_ref.at[pl.ds(0, (Y - 1) * share)]
    pltpu.make_async_copy(sent, sent, grid_send).wait()

    @pl.when(lo != ZLO - 1)
    def _():
        pltpu.make_async_copy(right_out, right_out, right_send).wait()

    @pl.when(lo != 0)
    def _():
        pltpu.make_async_copy(left_out, left_out, left_send).wait()

    @pl.when((lo == 0) | (lo == ZLO - 1))
    def _():
        sent = packed.at[:, pl.ds(0, DESTS - 1)]
        pltpu.make_async_copy(sent, sent, pack_send).wait()

    for begin, end in ((0, groups - 1), (groups - 1, groups)):
        high = Y * (end - begin) * tall
        at = slice(Y * begin * tall, Y * end * tall)
        if begin == 0:
            for group in range(begin, end):
                block = gathered.at[:, pl.ds(group * tall, tall)]
                pltpu.make_async_copy(block, block, plane_sem.at[group]).wait()
            left = jnp.concatenate(
                [
                    gathered[source * Y : (source + 1) * Y, : end * tall].reshape(high, 256)
                    for source in range(X * CORE)
                ],
                axis=1,
            )
            for tile in range(grid_lat // 512):
                lanes = slice(tile * 512, (tile + 1) * 512)
                term = jnp.dot(left, table[:, lanes], preferred_element_type=f32)
                spectra[at, lanes] = term.astype(bf16)
        else:
            for across in (0, 1, 2, 3, 6, 7, 4, 5):
                source = (x + X - across // CORE) % X * CORE + (core + CORE - across % CORE) % CORE
                part = pl.ds(source * Y, Y)
                block = gathered.at[part, pl.ds(begin * tall, tall)]
                pltpu.make_async_copy(block, block, plane_sem.at[begin + across]).wait()
                left = gathered[part, begin * tall : end * tall].reshape(high, 256)
                right = pl.ds(pl.multiple_of(source * 256, 256), 256)
                for tile in range(grid_lat // 512):
                    lanes = slice(tile * 512, (tile + 1) * 512)
                    term = jnp.dot(left, table[right, lanes], preferred_element_type=f32)
                    if across == 0:
                        late[:, lanes] = term
                    else:
                        late[:, lanes] += term
            spectra[at, :] = late[...].astype(bf16)
        for pair in range(pairs):
            low, top = max(0, pair - 1) * 128, min(pairs, pair + 2) * 128
            skip = 0 if pair else 128
            banded[at, pair * 128 : (pair + 1) * 128] = lax.dot_general(
                spectra[at, low:top],
                band[pair, :, skip : skip + top - low],
                (((1,), (1,)), ((), ())),
                preferred_element_type=f32,
            ).astype(bf16)
        for tile in range(grid_lat // 512):
            lanes = slice(tile * 512, (tile + 1) * 512)
            result = jnp.dot(mix[:, at], banded[at, lanes], preferred_element_type=f32)
            if begin == 0:
                mixed_early[:, lanes] = result
                continue
            result += mixed_early[:, lanes]
            for c in range(2):
                for field in range(fields):
                    row = (c * fields + field) * BLK
                    out_ref[c, field, :, lanes] = result[row : row + levels].astype(out_ref.dtype)

    sent = sending.at[pl.ds(0, PLANE - 1)]
    pltpu.make_async_copy(sent, sent, plane_send).wait()


def per_device(cotangent, wave_order, band_diagonal, band_lower, vertical_matrix):
    fields, levels, lat_local, lon_local = cotangent.shape
    rows = fields * levels
    grid_lat = lat_local * X * ZHI * CORE
    lon = lon_local * Y
    share = -(-rows // (Y * ROWS)) * ROWS
    steps = share // ROWS
    columns = 2 * wave_order.size
    half = columns // 2
    packed = (lat_local, ROWS * half // DESTS)
    tall = 4 * GROUP
    depth = -(-2 * share // tall) * tall
    owners = X * ZHI * CORE
    blocks = band_diagonal.shape[1]
    f32, bf16 = jnp.float32, jnp.bfloat16
    chain = pltpu.VMEM((steps * ROWS, lat_local, half), bf16)
    hbm = pl.BlockSpec(memory_space=pl.ANY)
    vmem = pl.BlockSpec(memory_space=pltpu.VMEM)
    dma = pltpu.SemaphoreType.DMA
    return pl.pallas_call(
        functools.partial(step_kernel, rows, share, steps),
        out_shape=pltpu.VMEM((2, fields, levels, grid_lat), bf16),
        in_specs=[hbm] * 5,
        out_specs=vmem,
        scratch_shapes=[
            pltpu.VMEM((1, wave_order.size), jnp.int32),
            pltpu.VMEM(band_diagonal.shape[1:], bf16),
            pltpu.VMEM(band_lower.shape[1:], bf16),
            pltpu.VMEM(vertical_matrix.shape, bf16),
            pltpu.VMEM((share, lat_local, lon), bf16),
            pltpu.VMEM((lon, columns), bf16),
            pltpu.VMEM((COARSE, columns), f32),
            pltpu.VMEM((COARSE, columns), f32),
            chain,
            chain,
            chain,
            chain,
            pltpu.VMEM((steps, DESTS) + packed, bf16),
            pltpu.VMEM((SIDES, ROWS * lat_local, half), f32),
            pltpu.VMEM((steps, ZHI) + packed, bf16),
            pltpu.VMEM((256, 128), f32),
            pltpu.VMEM((2, PLANE * depth, 128), f32),
            pltpu.VMEM((PLANE, depth, 256), bf16),
            pltpu.VMEM((PLANE, depth, 256), bf16),
            pltpu.VMEM((X * CORE * 256, grid_lat), bf16),
            pltpu.VMEM((owners, grid_lat), f32),
            pltpu.VMEM((owners, grid_lat), f32),
            pltpu.VMEM((lat_local, grid_lat), f32),
            pltpu.VMEM((lat_local, grid_lat), f32),
            pltpu.VMEM((blocks * BLK, 128), f32),
            pltpu.VMEM(((blocks - 1) * BLK, 128), f32),
            pltpu.VMEM((blocks // 2, 2 * BLK, 6 * BLK), bf16),
            pltpu.VMEM((128, 128), f32),
            pltpu.VMEM((2 * fields * BLK, Y * depth), bf16),
            pltpu.VMEM((Y * depth, grid_lat), bf16),
            pltpu.VMEM((Y * depth, grid_lat), bf16),
            pltpu.VMEM((2 * fields * BLK, grid_lat), f32),
            pltpu.VMEM((Y * tall, grid_lat), f32),
            dma((steps,)),
            dma,
            dma,
            dma((steps * ROWS,)),
            dma,
            dma((steps * ROWS,)),
            dma,
            dma((steps,)),
            dma,
            dma((depth // tall - 1 + X * CORE,)),
            dma((4,)),
        ],
        compiler_params=pltpu.CompilerParams(
            collective_id=0, has_side_effects=True, vmem_limit_bytes=54 << 20
        ),
    )(
        cotangent.reshape(rows, lat_local, lon_local),
        wave_order.reshape(1, -1),
        band_diagonal[0],
        band_lower[0],
        vertical_matrix,
    )[None]


def solution(mesh):
    return jax.shard_map(
        per_device,
        mesh=mesh,
        in_specs=(
            P(None, None, "lat", "lon"),
            P(),
            P(("lat", "lon"), None, None),
            P(("lat", "lon"), None, None),
            P(),
        ),
        out_specs=P(("lat", "lon"), None, None, None, None),
        check_vma=False,
    )
```

```python
import functools
import math

import jax
import jax.numpy as jnp
from jax import lax
from jax.experimental import pallas as pl
from jax.experimental.pallas import tpu as pltpu
from jax.sharding import PartitionSpec as P

BLK = 64
MESH = pl.DeviceIdType.MESH

X, ZHI, CORE, ZLO, Y = 4, 4, 2, 4, 4
PLANE = X * CORE * Y
GROUP = 4
SIDES, DESTS = 2, 8
GROUP_STEP = ((3, 3, 3, 3, 2, 2, 0, 0), (1, 1, 1, 1, 2, 2, 0, 0))
GROUP_PLACE = ((0, 1, 2, 3, 2, 3, 0, 1), (0, 1, 2, 3, 0, 1, 2, 3))
ROWS = 2
FIRST = 2
AHEAD = 2
LAG = 4
COARSE = 32
SKEW = 3


def place():
    lat, lon = lax.axis_index("lat"), lax.axis_index("lon")
    return lat // (ZHI * CORE), lat // CORE % ZHI, lat % CORE, lon // Y, lon % Y


def device(x, hi, core, lo, y):
    return ((x * ZHI + hi) * CORE + core, lo * Y + y)


def cosine(phase, period):
    quarter = period // 4
    turns = jnp.floor(phase * (1.0 / quarter) + 0.5)
    angle = (phase - turns * quarter) * (2.0 * math.pi / period)
    square = angle * angle
    even = 1.0 + square * (
        -1 / 2 + square * (1 / 24 + square * (-1 / 720 + square * (1 / 40320)))
    )
    odd = angle * (
        1.0 + square * (-1 / 6 + square * (1 / 120 + square * (-1 / 5040 + square * (1 / 362880))))
    )
    turn = turns.astype(jnp.int32) & 3
    value = jnp.where((turn & 1) == 1, odd, even)
    return jnp.where((turn == 1) | (turn == 2), -value, value)


def slots_of_columns(hi, column):
    width = 2 * PLANE
    side, dest, plane = column // (DESTS * width), column // width % DESTS, column % PLANE
    step = jnp.where(dest < 4, jnp.where(side == 0, 3, 1), jnp.where(dest < 6, 2, 0))
    low_side = jnp.where(dest < 4, dest, jnp.where(dest < 6, dest - 2, dest - 6))
    lo = jnp.where(side == 0, low_side, dest % 4)
    lo = jnp.where((side == 1) & (dest >= 6), dest - 4, lo)
    to_hi = (hi + step) % ZHI
    x, core, y = plane // (CORE * Y), plane // Y % CORE, plane % Y
    return (((x * ZHI + to_hi) * CORE + core) * ZLO + lo) * Y + y


def waves_of_columns(wave_ref, hi, columns):
    slots = wave_ref.shape[1]
    slot = slots_of_columns(hi, lax.broadcasted_iota(jnp.int32, (1, columns), 1))
    wave = jnp.broadcast_to(wave_ref[...], (8, slots))
    pick = lax.broadcasted_iota(jnp.int32, (slots, columns), 0) == slot
    pick = jnp.where(pick, 1.0, 0.0).astype(jnp.bfloat16)

    def picked(digits):
        digits = digits.astype(jnp.float32).astype(jnp.bfloat16)
        return jnp.dot(digits, pick, preferred_element_type=jnp.float32)[:1]

    return picked(wave // 16) * 16.0 + picked(wave % 16)


def step_kernel(
    rows, share, steps,
    grid_ref, wave_hbm, diagonal_hbm, lower_hbm, vertical_hbm, out_ref,
    wave_ref, diagonal_ref, lower_ref, vertical_ref,
    grid, basis, u_ref, v_ref, right_in, left_in, right_out, left_out, packed, total,
    parts, wide, spread, sending, gathered,
    table, base_cos, base_sin, near_cos, near_sin,
    diagonal, lower, band, levels_pad, mix, spectra, banded, mixed_early, late,
    grid_sem, grid_send, right_send, right_recv, left_send, left_recv,
    pack_send, part_sem, plane_send, plane_sem, own_sem,
):
    x, hi, core, lo, y = place()
    mine = (x * CORE + core) * Y + y
    lat_local, lon_local = grid_ref.shape[1:]
    half = basis.shape[1] // 2
    width = half // DESTS
    f32, bf16 = jnp.float32, jnp.bfloat16

    def peer(offset):
        other = (mine + offset) % PLANE
        return other, device(other // (CORE * Y), hi, other // Y % CORE, lo, other % Y)

    own = [
        pltpu.make_async_copy(there, here, own_sem.at[number])
        for number, (there, here) in enumerate(
            (
                (wave_hbm, wave_ref),
                (diagonal_hbm, diagonal_ref),
                (lower_hbm, lower_ref),
                (vertical_hbm, vertical_ref),
            )
        )
    ]
    barrier = pltpu.get_barrier_semaphore()

    def greet_line(offset, carry):
        z = (hi * ZLO + lo + offset) % (ZHI * ZLO)
        pl.semaphore_signal(
            barrier, inc=1, device_id=device(x, z // ZLO, core, z % ZLO, y), device_id_type=MESH
        )
        return carry

    def greet_plane(offset, carry):
        pl.semaphore_signal(barrier, inc=1, device_id=peer(offset)[1], device_id_type=MESH)
        return carry

    lax.fori_loop(1, ZHI * ZLO, greet_line, 0)
    lax.fori_loop(1, PLANE, greet_plane, 0)
    for copy in own:
        copy.start()
    pl.semaphore_wait(barrier, ZHI * ZLO - 1 + PLANE - 1)

    def first_row(owner):
        return jnp.minimum(owner * share, rows - share)

    def grid_copies(step):
        columns = pl.ds(pl.multiple_of(y * lon_local, lon_local), lon_local)
        target = grid.at[pl.ds(step * ROWS, ROWS), :, columns]
        for offset in range(1, Y):
            owner = (y + offset) % Y
            pltpu.make_async_remote_copy(
                src_ref=grid_ref.at[pl.ds(first_row(owner) + step * ROWS, ROWS)],
                dst_ref=target,
                send_sem=grid_send,
                recv_sem=grid_sem.at[step],
                device_id=device(x, hi, core, lo, owner),
                device_id_type=MESH,
            ).start()
        pltpu.make_async_copy(
            grid_ref.at[pl.ds(first_row(y) + step * ROWS, ROWS)], target, grid_sem.at[step]
        ).start()

    for step in range(FIRST):
        grid_copies(step)

    own[0].wait()
    waves = waves_of_columns(wave_ref, hi, basis.shape[1])
    column = lax.broadcasted_iota(jnp.int32, (1, basis.shape[1]), 1)
    sine = jnp.where(column // PLANE % 2 == 1, 1.0, 0.0)
    lon, grid_lon = basis.shape[0], basis.shape[0] * ZLO
    coarse, fine = u_ref.shape[0], lon // u_ref.shape[0]
    scale = math.sqrt(2.0 / grid_lon)
    first = (lo * lon + fine * lax.broadcasted_iota(jnp.int32, (coarse, 1), 0)).astype(f32)
    base = waves * first - sine * (grid_lon // 4)
    u_ref[...] = cosine(base, grid_lon) * scale
    v_ref[...] = cosine(base + grid_lon // 4, grid_lon) * scale
    near = waves * lax.broadcasted_iota(jnp.int32, (fine, 1), 0).astype(f32)
    fine_cos, fine_sin = cosine(near, grid_lon), cosine(near - grid_lon // 4, grid_lon)

    def fill(a, carry):
        piece = u_ref[pl.ds(a, 1), :] * fine_cos + v_ref[pl.ds(a, 1), :] * fine_sin
        basis[pl.ds(pl.multiple_of(a * fine, fine), fine), :] = piece.astype(bf16)
        return carry

    lax.fori_loop(0, coarse, fill, 0)
    for copy in own[1:]:
        copy.wait()
    for step in range(FIRST, AHEAD):
        grid_copies(step)

    def product(step, side):
        left = grid[pl.ds(step * ROWS, ROWS)].reshape(ROWS * lat_local, grid.shape[2])
        return jnp.dot(
            left, basis[:, side * half : (side + 1) * half], preferred_element_type=f32
        )

    def hand_out(step, side):
        for pair in range(DESTS // 2):
            lanes = slice(pair * 2 * width, (pair + 1) * 2 * width)
            top, low = total[side, :lat_local, lanes], total[side, lat_local:, lanes]
            for odd in range(2):
                part = slice(odd * width, (odd + 1) * width)
                packed[step, pair * 2 + odd] = jnp.concatenate(
                    [top[:, part], low[:, part]], axis=1
                ).astype(bf16)
        own_lo = ZLO - 1 if side else 0
        for dest in range(DESTS):
            to_hi = (hi + GROUP_STEP[side][dest]) % ZHI
            to_lo = GROUP_PLACE[side][dest]
            if GROUP_STEP[side][dest] == 0 and to_lo == own_lo:
                pltpu.make_async_copy(
                    packed.at[step, dest], parts.at[step, hi], part_sem.at[step]
                ).start()
            else:
                pltpu.make_async_remote_copy(
                    src_ref=packed.at[step, dest],
                    dst_ref=parts.at[step, hi],
                    send_sem=pack_send,
                    recv_sem=part_sem.at[step],
                    device_id=device(x, to_hi, core, to_lo, y),
                    device_id_type=MESH,
                ).start()

    def chain(step, side):
        arrived, leaving = (right_in, right_out) if side else (left_in, left_out)
        send_sem, recv_sem = (right_send, right_recv) if side else (left_send, left_recv)
        first, last = (0, ZLO - 1) if side else (ZLO - 1, 0)
        row = step % ROWS
        sums = total.at[side, pl.ds(pl.multiple_of(row * lat_local, lat_local), lat_local)]

        @pl.when(row == 0)
        def _():
            total[side] = product(step // ROWS, side)

        @pl.when(lo != first)
        def _():
            pltpu.make_async_copy(arrived.at[step], arrived.at[step], recv_sem.at[step]).wait()
            sums[...] += arrived[step].astype(f32)

        @pl.when(lo != last)
        def _():
            leaving[step] = sums[...].astype(bf16)
            pltpu.make_async_remote_copy(
                src_ref=leaving.at[step],
                dst_ref=arrived.at[step],
                send_sem=send_sem,
                recv_sem=recv_sem.at[step],
                device_id=device(x, hi, core, lo + (1 if side else -1), y),
                device_id_type=MESH,
            ).start()

        @pl.when((lo == last) & (row == ROWS - 1))
        def _():
            hand_out(step // ROWS, side)

    span = ZHI * lat_local
    depth = sending.shape[1]
    tall = 4 * GROUP

    def turn(step):
        pltpu.make_async_copy(parts.at[step], parts.at[step], part_sem.at[step]).wait()
        wide[:span, :] = parts[step].reshape(span, 128).astype(f32)
        turned = wide[...].T
        for group in range(4):
            for part in range(2):
                spread[part, pl.ds(4 * step + group, PLANE, stride=depth), :] = turned[
                    group * PLANE : (group + 1) * PLANE, part * 128 : (part + 1) * 128
                ]

    groups = depth // tall

    def arrival(group, offset):
        other = (mine + offset) % PLANE
        across = (other // (CORE * Y) + X - x) % X * CORE + (other // Y % CORE + CORE - core) % CORE
        return plane_sem.at[group + group // (groups - 1) * across]

    def through_plane(group):
        at = pl.ds(pl.multiple_of(group * tall, tall), tall)

        def narrow(other):
            begin = pl.multiple_of(other * depth + group * tall, tall)
            for part in range(2):
                sending[other, at, part * 128 : (part + 1) * 128] = spread[
                    part, pl.ds(begin, tall), :
                ].astype(bf16)

        def send(offset, carry):
            other, where = peer(offset)
            narrow(other)
            pltpu.make_async_remote_copy(
                src_ref=sending.at[other, at],
                dst_ref=gathered.at[mine, at],
                send_sem=plane_send,
                recv_sem=arrival(group, offset),
                device_id=where,
                device_id_type=MESH,
            ).start()
            return carry

        lax.fori_loop(1, PLANE, send, 0)
        narrow(mine)
        pltpu.make_async_copy(
            sending.at[mine, at], gathered.at[mine, at], arrival(group, 0)
        ).start()

    grid_lat = table.shape[1]
    blocks = diagonal_ref.shape[0]
    fields, levels = vertical_ref.shape[:2]
    owners = X * ZHI * CORE
    pairs = blocks // 2

    def start_meridional():
        scale = math.sqrt(2.0 / grid_lat)
        mode = lax.broadcasted_iota(jnp.int32, (1, grid_lat), 1).astype(f32)
        base = 2 * lat_local * lax.broadcasted_iota(jnp.int32, (owners, 1), 0)
        base = base.astype(f32) * mode
        base_cos[...] = cosine(base, 4 * grid_lat) * scale
        base_sin[...] = cosine(base - grid_lat, 4 * grid_lat) * scale
        near = (2 * lax.broadcasted_iota(jnp.int32, (lat_local, 1), 0) + 1).astype(f32) * mode
        near_cos[...] = cosine(near, 4 * grid_lat)
        near_sin[...] = cosine(near - grid_lat, 4 * grid_lat)
        wide[...] = jnp.zeros_like(wide)
        for row in range(4 * steps, depth):
            for part in range(2):
                spread[part, pl.ds(row, PLANE, stride=depth), :] = jnp.zeros((PLANE, 128), f32)
        for source in range(X * CORE):
            table[source * 256 + span : (source + 1) * 256, :] = jnp.zeros(
                (256 - span, grid_lat), bf16
            )

    def meridional(owner):
        to_x, to_hi, to_core = owner // (ZHI * CORE), owner // CORE % ZHI, owner % CORE
        at = (to_x * CORE + to_core) * 256 + to_hi * lat_local
        piece = base_cos[pl.ds(owner, 1), :] * near_cos[...]
        piece -= base_sin[pl.ds(owner, 1), :] * near_sin[...]
        table[pl.ds(pl.multiple_of(at, 16), lat_local), :] = piece.astype(bf16)

    def squares(lanes):
        tile = pl.ds(pl.multiple_of(lanes * 128, 128), 128)
        for flat, square in ((diagonal_ref, diagonal), (lower_ref, lower)):
            piece = flat[:, tile].astype(f32)
            square[pl.ds(2 * lanes, flat.shape[0], stride=BLK), :] = piece
            square[pl.ds(2 * lanes + 1, flat.shape[0], stride=BLK), :] = pltpu.roll(piece, 64, 1)

    def square(ref, block):
        return ref[pl.ds(pl.multiple_of(block * BLK, BLK), BLK), :][:, :BLK]

    def band_pair(pair):
        one, two = 2 * pair, 2 * pair + 1
        empty = jnp.zeros((BLK, BLK), f32)
        before = jnp.where(pair > 0, square(lower, jnp.maximum(one - 1, 0)), 0.0)
        after = square(lower, jnp.minimum(two, blocks - 2)).T
        after = jnp.where(two < blocks - 1, after, 0.0)
        inner = square(lower, one)
        top = (empty, before, square(diagonal, one), inner.T, empty, empty)
        low = (empty, empty, inner, square(diagonal, two), after, empty)
        band[pair, :BLK, :] = jnp.concatenate(top, axis=1).astype(bf16)
        band[pair, BLK:, :] = jnp.concatenate(low, axis=1).astype(bf16)

    held = mix.shape[1]
    early = depth - tall

    def mixing():
        at = lax.broadcasted_iota(jnp.int32, (1, held), 1)
        rest = at - Y * early
        owner = jnp.where(rest < 0, at // early, rest // tall)
        within = jnp.where(rest < 0, at % early, early + rest % tall)
        row = jnp.minimum(owner * share, rows - share) + within // 2
        fresh = (row >= owner * share) & (within < 2 * share)
        level = lax.broadcasted_iota(jnp.int32, (BLK, 1), 0)
        for field in range(fields):
            levels_pad[...] = jnp.zeros_like(levels_pad)
            levels_pad[:levels, :levels] = vertical_ref[field].astype(f32)
            turned = levels_pad[...].T[:BLK, :].astype(bf16)
            pick = (row == field * levels + level) & (level < levels) & fresh
            pick = jnp.where(pick, 1.0, 0.0).astype(bf16)
            pick = jnp.concatenate([pick, jnp.zeros((128 - BLK, held), bf16)], axis=0)
            mixed = jnp.dot(turned, pick, preferred_element_type=f32)
            for c in range(2):
                part = (c * fields + field) * BLK
                mix[part : part + BLK, :] = jnp.where(at % 2 == c, mixed, 0.0).astype(bf16)

    fill_steps = SKEW * (ZLO - 1)
    count = (steps + LAG) * ROWS + fill_steps
    duties = (
        (start_meridional, 10, 1, 0),
        (mixing, 11, 1, 0),
        (squares, 12, BLK // 2, 2),
        (meridional, 11, owners, 1),
        (band_pair, 12 + BLK // 4, pairs, 1),
    )

    def one(step, carry):
        @pl.when((step % ROWS == 0) & (step // ROWS + AHEAD < steps))
        def _():
            grid_copies(step // ROWS + AHEAD)

        first = step - SKEW * jnp.minimum(lo, ZLO - 1 - lo)

        @pl.when((first >= 0) & (first < steps * ROWS) & (first % ROWS == 0))
        def _():
            block = grid.at[pl.ds(first, ROWS)]
            pltpu.make_async_copy(block, block, grid_sem.at[first // ROWS]).wait()

        for side, here in ((1, lo < ZLO // 2), (0, lo >= 0), (1, lo >= ZLO // 2)):
            at = step - SKEW * (lo if side else ZLO - 1 - lo)

            @pl.when(here & (at >= 0) & (at < steps * ROWS))
            def _():
                chain(at, side)

        ahead = step - fill_steps - (ROWS - 1) - LAG * ROWS
        done = ahead // ROWS

        @pl.when((ahead >= 0) & (ahead % ROWS == 0))
        def _():
            turn(done)

            @pl.when((done % GROUP == GROUP - 1) | (done == steps - 1))
            def _():
                through_plane(done // GROUP)

        for duty, begin, number, each in duties:
            if each:

                @pl.when((step >= begin) & (step < begin + number // each))
                def _():
                    for extra in range(each):
                        duty((step - begin) * each + extra)
            else:

                @pl.when(step == begin)
                def _():
                    duty()

        return carry

    lax.fori_loop(0, count, one, 0)

    sent = grid_ref.at[pl.ds(0, (Y - 1) * share)]
    pltpu.make_async_copy(sent, sent, grid_send).wait()

    @pl.when(lo != ZLO - 1)
    def _():
        pltpu.make_async_copy(right_out, right_out, right_send).wait()

    @pl.when(lo != 0)
    def _():
        pltpu.make_async_copy(left_out, left_out, left_send).wait()

    @pl.when((lo == 0) | (lo == ZLO - 1))
    def _():
        sent = packed.at[:, pl.ds(0, DESTS - 1)]
        pltpu.make_async_copy(sent, sent, pack_send).wait()

    for begin, end in ((0, groups - 1), (groups - 1, groups)):
        high = Y * (end - begin) * tall
        at = slice(Y * begin * tall, Y * end * tall)
        if begin == 0:
            for group in range(begin, end):
                block = gathered.at[:, pl.ds(group * tall, tall)]
                pltpu.make_async_copy(block, block, plane_sem.at[group]).wait()
            left = jnp.concatenate(
                [
                    gathered[source * Y : (source + 1) * Y, : end * tall].reshape(high, 256)
                    for source in range(X * CORE)
                ],
                axis=1,
            )
            for tile in range(grid_lat // 512):
                lanes = slice(tile * 512, (tile + 1) * 512)
                term = jnp.dot(left, table[:, lanes], preferred_element_type=f32)
                spectra[at, lanes] = term.astype(bf16)
        else:
            for across in (0, 1, 2, 3, 6, 7, 4, 5):
                source = (x + X - across // CORE) % X * CORE + (core + CORE - across % CORE) % CORE
                part = pl.ds(source * Y, Y)
                block = gathered.at[part, pl.ds(begin * tall, tall)]
                pltpu.make_async_copy(block, block, plane_sem.at[begin + across]).wait()
                left = gathered[part, begin * tall : end * tall].reshape(high, 256)
                right = pl.ds(pl.multiple_of(source * 256, 256), 256)
                for tile in range(grid_lat // 512):
                    lanes = slice(tile * 512, (tile + 1) * 512)
                    term = jnp.dot(left, table[right, lanes], preferred_element_type=f32)
                    if across == 0:
                        late[:, lanes] = term
                    else:
                        late[:, lanes] += term
            spectra[at, :] = late[...].astype(bf16)
        for pair in range(pairs):
            low, top = max(0, pair - 1) * 128, min(pairs, pair + 2) * 128
            skip = 0 if pair else 128
            banded[at, pair * 128 : (pair + 1) * 128] = lax.dot_general(
                spectra[at, low:top],
                band[pair, :, skip : skip + top - low],
                (((1,), (1,)), ((), ())),
                preferred_element_type=f32,
            ).astype(bf16)
        for tile in range(grid_lat // 512):
            lanes = slice(tile * 512, (tile + 1) * 512)
            result = jnp.dot(mix[:, at], banded[at, lanes], preferred_element_type=f32)
            if begin == 0:
                mixed_early[:, lanes] = result
                continue
            result += mixed_early[:, lanes]
            for c in range(2):
                for field in range(fields):
                    row = (c * fields + field) * BLK
                    out_ref[c, field, :, lanes] = result[row : row + levels].astype(out_ref.dtype)

    sent = sending.at[pl.ds(0, PLANE - 1)]
    pltpu.make_async_copy(sent, sent, plane_send).wait()


def per_device(cotangent, wave_order, band_diagonal, band_lower, vertical_matrix):
    fields, levels, lat_local, lon_local = cotangent.shape
    rows = fields * levels
    grid_lat = lat_local * X * ZHI * CORE
    lon = lon_local * Y
    share = -(-rows // (Y * ROWS)) * ROWS
    steps = share // ROWS
    columns = 2 * wave_order.size
    half = columns // 2
    packed = (lat_local, ROWS * half // DESTS)
    tall = 4 * GROUP
    depth = -(-2 * share // tall) * tall
    owners = X * ZHI * CORE
    blocks = band_diagonal.shape[1]
    f32, bf16 = jnp.float32, jnp.bfloat16
    chain = pltpu.VMEM((steps * ROWS, lat_local, half), bf16)
    hbm = pl.BlockSpec(memory_space=pl.ANY)
    vmem = pl.BlockSpec(memory_space=pltpu.VMEM)
    dma = pltpu.SemaphoreType.DMA
    return pl.pallas_call(
        functools.partial(step_kernel, rows, share, steps),
        out_shape=pltpu.VMEM((2, fields, levels, grid_lat), bf16),
        in_specs=[hbm] * 5,
        out_specs=vmem,
        scratch_shapes=[
            pltpu.VMEM((1, wave_order.size), jnp.int32),
            pltpu.VMEM(band_diagonal.shape[1:], bf16),
            pltpu.VMEM(band_lower.shape[1:], bf16),
            pltpu.VMEM(vertical_matrix.shape, bf16),
            pltpu.VMEM((share, lat_local, lon), bf16),
            pltpu.VMEM((lon, columns), bf16),
            pltpu.VMEM((COARSE, columns), f32),
            pltpu.VMEM((COARSE, columns), f32),
            chain,
            chain,
            chain,
            chain,
            pltpu.VMEM((steps, DESTS) + packed, bf16),
            pltpu.VMEM((SIDES, ROWS * lat_local, half), f32),
            pltpu.VMEM((steps, ZHI) + packed, bf16),
            pltpu.VMEM((256, 128), f32),
            pltpu.VMEM((2, PLANE * depth, 128), f32),
            pltpu.VMEM((PLANE, depth, 256), bf16),
            pltpu.VMEM((PLANE, depth, 256), bf16),
            pltpu.VMEM((X * CORE * 256, grid_lat), bf16),
            pltpu.VMEM((owners, grid_lat), f32),
            pltpu.VMEM((owners, grid_lat), f32),
            pltpu.VMEM((lat_local, grid_lat), f32),
            pltpu.VMEM((lat_local, grid_lat), f32),
            pltpu.VMEM((blocks * BLK, 128), f32),
            pltpu.VMEM((blocks * BLK, 128), f32),
            pltpu.VMEM((blocks // 2, 2 * BLK, 6 * BLK), bf16),
            pltpu.VMEM((128, 128), f32),
            pltpu.VMEM((2 * fields * BLK, Y * depth), bf16),
            pltpu.VMEM((Y * depth, grid_lat), bf16),
            pltpu.VMEM((Y * depth, grid_lat), bf16),
            pltpu.VMEM((2 * fields * BLK, grid_lat), f32),
            pltpu.VMEM((Y * tall, grid_lat), f32),
            dma((steps,)),
            dma,
            dma,
            dma((steps * ROWS,)),
            dma,
            dma((steps * ROWS,)),
            dma,
            dma((steps,)),
            dma,
            dma((depth // tall - 1 + X * CORE,)),
            dma((4,)),
        ],
        compiler_params=pltpu.CompilerParams(
            collective_id=0, has_side_effects=True, vmem_limit_bytes=54 << 20
        ),
    )(
        cotangent.reshape(rows, lat_local, lon_local),
        wave_order.reshape(1, -1),
        band_diagonal[0],
        band_lower[0],
        vertical_matrix,
    )[None]


def solution(mesh):
    return jax.shard_map(
        per_device,
        mesh=mesh,
        in_specs=(
            P(None, None, "lat", "lon"),
            P(),
            P(("lat", "lon"), None, None),
            P(("lat", "lon"), None, None),
            P(),
        ),
        out_specs=P(("lat", "lon"), None, None, None, None),
        check_vma=False,
    )
```
